32 devices in a mesh: grp: 2 (over x), row: 8 (over z, y), col: 2 (over core).
Axes of the slice: x: 2, y: 2, z: 4, core: 2. Of those that a mesh axis runs over, the one named last changes fastest.
Arguments:
- alignment_left: bfloat16 [128, 32, 256], P('col', None, ('grp', 'row')), parts along dimension 2, may hold values from -10 to 10
- alignment_right: bfloat16 [128, 32, 256], P('col', None, ('grp', 'row')), parts along dimension 2, may hold values from -10 to 10
- weight: bfloat16 [1024, 128], replicated, may hold values from -0.1875 to 0.1875
- pairwise_bias: bfloat16 [128], replicated, may hold values from -3 to 3
- cotangent: bfloat16 [256, 128, 128], P(('grp', 'row'), 'col'), parts along dimension 0, may hold values from -6 to 6
Outputs:
- pair_update: bfloat16 [256, 128, 128], P(('grp', 'row'), 'col'), parts along dimension 0
- grad_left: float32 [128, 32, 256], P('col', None, ('grp', 'row')), parts along dimension 2
- grad_right: float32 [128, 32, 256], P('col', None, ('grp', 'row')), parts along dimension 2
- grad_weight: float32 [2048, 128], P('grp'), parts along dimension 0
- grad_bias: float32 [256], P('grp'), parts along dimension 0
The draws below stay inside these ranges and needn't reach their ends.
There are 2 independent parts, one for each index of `grp`. The reference program is written for one: setup_inputs(seed, part) draws one part's arguments, and reference() takes and returns one part's arrays. A program takes and returns all parts, laid end to end along the dimension named above; an argument that names none is the same for every part. Nothing has to cross between parts.
All inputs are finite; a program needn't handle non-finite values.
Results may differ from the reference program's by a relative error of at most 0.0034.
Values may be sent and summed in bfloat16 or wider, within the bound.
A program may use at most 128 MiB of HBM per device.

```python
import jax
import jax.numpy as jnp
from jax import lax

CHANNEL_COUNT = 32
CZ = 128
SEQUENCE_COUNT = 128
RESIDUE_COUNT = 128


def raised(values, stream_key, source, target, blocks, factor):
    owner, partner = [(jnp.arange(values.shape[axis_at]) // (values.shape[axis_at] // blocks)).reshape([-1 if axis == axis_at else 1 for axis in range(values.ndim)]) for axis_at in (source, target)]
    chosen = jax.random.permutation(stream_key, blocks)[partner]
    strong = (owner == chosen) | (owner == (partner + blocks // 2) % blocks)
    return jnp.where(strong, factor * values, values)


def level_of(rng, extent, shards, low, largest):
    loudness = 1.0
    for dim, shards_of in shards:
        draws = jax.random.uniform(jax.random.fold_in(jax.random.fold_in(rng, 6), dim), (shards_of,), jnp.float32, low / len(shards), largest / len(shards))
        loudness = loudness * jnp.repeat(jnp.exp(draws), extent[dim] // shards_of).reshape((-1,) + (1,) * (len(extent) - 1 - dim))
    return loudness


def bell_draw(stream_key, dims, width, bound, pieces=(), held_as=jnp.bfloat16):
    result = jax.random.normal(stream_key, dims, jnp.float32) * width
    if len(pieces) > 0:
        result = level_of(stream_key, dims, pieces, -0.22, 0.18) * result
    return jnp.clip(result, min=-bound, max=bound).astype(held_as)


def bell_draw_with(own_key, extent, spread, most, shards, heavy, kind=jnp.bfloat16):
    array = spread * jax.random.normal(own_key, extent, jnp.float32)
    if shards:
        array = array * level_of(own_key, extent, shards, -0.22, 0.18)
    return jnp.clip(raised(array, jax.random.fold_in(own_key, 3), *heavy), -most, most).astype(kind)


def setup_inputs(seed: int = 0, part: int = 0) -> dict:
    splits = jax.random.split(jax.random.key(seed), 6)
    part_keys = jax.random.split(jax.random.fold_in(splits[5], part), 6)
    alignment_left = bell_draw(part_keys[0], (SEQUENCE_COUNT, CHANNEL_COUNT, RESIDUE_COUNT), 2.0, 10.0, ((0, 2), (2, 8)))
    alignment_right = bell_draw(part_keys[1], (SEQUENCE_COUNT, CHANNEL_COUNT, RESIDUE_COUNT), 2.0, 10.0, ((0, 2), (2, 8)))
    weight = bell_draw(splits[2], (CHANNEL_COUNT * CHANNEL_COUNT, CZ), (CHANNEL_COUNT * CHANNEL_COUNT) ** -0.5, 0.1875)
    pairwise_bias = bell_draw(splits[3], (CZ,), 0.5, 3.0)
    cotangent = bell_draw_with(part_keys[4], (RESIDUE_COUNT, RESIDUE_COUNT, CZ), 1.0, 6.0, ((0, 8), (1, 2)), (0, 1, 8, 2.0))
    return {"alignment_left": alignment_left, "alignment_right": alignment_right, "weight": weight, "pairwise_bias": pairwise_bias, "cotangent": cotangent}


def reference(alignment_left, alignment_right, weight, pairwise_bias, cotangent):
    sequence_total, channel_count, residue_count = alignment_left.shape
    inv_seqs = 1.0 / sequence_total
    block_height = min(16, residue_count)
    right_widened = alignment_right.astype(jnp.float32)
    pair_dim = weight.shape[1]

    def one_block(state_tuple, first_row):
        weight_acc, cols_acc = state_tuple
        left_portion = lax.dynamic_slice_in_dim(alignment_left, first_row, block_height, 2).astype(jnp.float32)
        grad_part = lax.dynamic_slice_in_dim(cotangent, first_row, block_height, 0)
        outer_tile = jnp.einsum("sci,sdj->ijcd", left_portion, right_widened) * inv_seqs
        outer_tile = outer_tile.astype(jnp.bfloat16).reshape(block_height * residue_count, channel_count * channel_count)
        projected = jnp.dot(outer_tile, weight, preferred_element_type=jnp.float32) + pairwise_bias.astype(jnp.float32)
        projected = projected.astype(jnp.bfloat16).reshape(block_height, residue_count, pair_dim)
        flat_grad = grad_part.reshape(block_height * residue_count, pair_dim)
        grad_outer = jnp.dot(flat_grad, weight.T, preferred_element_type=jnp.float32).astype(jnp.bfloat16)
        weight_acc = weight_acc + jnp.dot(outer_tile.T, flat_grad, preferred_element_type=jnp.float32)
        grad_wide = grad_outer.reshape(block_height, residue_count, channel_count, channel_count).astype(jnp.float32)
        rows_term = jnp.einsum("ijcd,sdj->sci", grad_wide, right_widened) * inv_seqs
        cols_acc = cols_acc + jnp.einsum("ijcd,sci->sdj", grad_wide, left_portion) * inv_seqs
        return (weight_acc, cols_acc), (projected, rows_term)

    starts = jnp.arange(residue_count // block_height, dtype=jnp.int32) * block_height
    initial = (jnp.zeros((channel_count * channel_count, pair_dim), jnp.float32), jnp.zeros((sequence_total, channel_count, residue_count), jnp.float32))
    (weight_acc, cols_acc), (projected, rows_term) = lax.scan(one_block, initial, starts)
    pair_update = projected.reshape(residue_count, residue_count, pair_dim)
    grad_left = jnp.moveaxis(rows_term, 0, 2).reshape(sequence_total, channel_count, residue_count)
    grad_bias = jnp.sum(cotangent.astype(jnp.float32), axis=(0, 1)) / residue_count
    return pair_update, grad_left, cols_acc, weight_acc / residue_count, grad_bias
```

```python
import functools

import jax
import jax.numpy as jnp
from jax import lax
from jax.experimental import pallas as pl
from jax.experimental.pallas import tpu as pltpu
from jax.sharding import PartitionSpec as P

MESH = pl.DeviceIdType.MESH
F32, BF16 = jnp.float32, jnp.bfloat16


def dot(a, b, ca=1, cb=0):
    return lax.dot_general(a, b, (((ca,), (cb,)), ((), ())), preferred_element_type=F32)


def kernel(
    rows, own, left_ref, right_ref, w_ref, bias_ref, cot_ref,
    pair_ref, gl_ref, gr_ref, gw_ref, gb_ref,
    lbuf, rbuf, perm, lt, wt, bd, scr, grs, rs, os, gsend, gbuf,
    gacc, wsib, wsend, wr, agbuf, glacc, glsib, bsend, bbuf,
    lsem, rssem, rsem, gssem, gsem, wsem, wssem, wrsem, assem, asem, fsem, glsem, bssem, bsem,
):
    g, r, k = lax.axis_index("grp"), lax.axis_index("row"), lax.axis_index("col")
    sib = 1 - k
    half_s, wide = left_ref.shape
    ires = cot_ref.shape[0]
    chan = wide // ires
    d2n = chan // 2
    seqs = 2 * half_s
    inv_seqs = 1.0 / seqs
    owners = rows // 2
    per = 64 // ires
    blocks = owners // per
    kt, ol = r // owners, r % owners
    stride = rows // own
    lanes = d2n * 128

    def remote(src, dst, ss, rs_, row, col):
        return pltpu.make_async_remote_copy(
            src_ref=src, dst_ref=dst, send_sem=ss, recv_sem=rs_,
            device_id=(g, row, col), device_id_type=MESH)

    def landed(ref, sem):
        pltpu.make_async_copy(ref, ref, sem).wait()

    barrier = pltpu.get_barrier_semaphore()

    @pl.loop(1, 2 * rows)
    def _(t):
        q = (2 * r + k + t) % (2 * rows)
        pl.semaphore_signal(barrier, inc=1, device_id=(g, q // 2, q % 2), device_id_type=MESH)

    pl.semaphore_wait(barrier, 2 * rows - 1)

    left_copy = remote(left_ref, lbuf.at[k], lsem.at[0], lsem.at[1], r, sib)
    left_copy.start()

    def right_copy(t):
        return remote(right_ref, rbuf.at[ol, k], rssem.at[t], rsem.at[ol, k], (r + t) % rows, kt)

    @pl.when(kt == k)
    def _():
        pltpu.make_async_copy(right_ref, rbuf.at[ol, k], rsem.at[ol, k]).start()

    @pl.when(kt != k)
    def _():
        remote(right_ref, rbuf.at[ol, k], rssem.at[0], rsem.at[ol, k], r, sib).start()

    @pl.loop(1, rows)
    def _(t):
        right_copy(t).start()

    bsend[...] = jnp.broadcast_to(
        jnp.sum(cot_ref[...].astype(F32), axis=(0, 1)).reshape(1, -1), bsend.shape)

    def bias_copy(t):
        q = (2 * r + k + t) % (2 * rows)
        return remote(bsend, bbuf.at[2 * r + k], bssem.at[t], bsem.at[2 * r + k], q // 2, q % 2)

    @pl.loop(1, 2 * rows)
    def _(t):
        bias_copy(t).start()

    bbuf[2 * r + k] = bsend[...]
    lbuf[k] = left_ref[...]

    dd = 128 // ires
    pm = lax.broadcasted_iota(jnp.int32, perm.shape, 0)
    pn = lax.broadcasted_iota(jnp.int32, perm.shape, 1)
    goal = (pm % 128 // ires) * 64 + (pm // 128) * ires + pm % ires
    perm[...] = jnp.where(goal == pn, 1.0, 0.0).astype(BF16)
    wt[...] = w_ref[...].astype(F32).T.astype(BF16)
    bd[...] = jnp.zeros(bd.shape, BF16)

    def fill_bd(b):
        for i in range(ires):
            piece = cot_ref[i, pl.ds(pl.multiple_of(b * 64, 64), 64), :]
            bd[i * 128 : i * 128 + 64, 0:128] = piece
            bd[i * 128 + 64 : i * 128 + 128, 128:256] = piece

    def each_block(fn):
        if blocks == 1:
            fn(0)
        else:
            pl.loop(0, blocks)(fn)

    def grads(b):
        fill_bd(b)

        @pl.loop(0, ires // 2)
        def _(p):
            res = dot(w_ref[...], bd[pl.ds(pl.multiple_of(p * 256, 256), 256), :], 1, 1)
            for u in range(2):
                scr[u] = res[:, u * 128 : u * 128 + 128]
            for u in range(2):
                at = pl.multiple_of((2 * p + u) * chan, chan)
                for q in range(d2n):
                    grs[b, pl.ds(at, chan), q * 128 : q * 128 + 128] = scr[
                        u, pl.ds(q, chan, stride=d2n), :].astype(BF16)

    each_block(grads)

    left_copy.wait_recv()
    lm = lbuf[...].reshape(seqs, wide)
    lt[...] = lm.astype(F32).T.astype(BF16)

    def right_back(o, h):
        return remote(gsend.at[o, h], gbuf.at[r], gssem.at[o, h], gsem.at[r], k * owners + o, h)

    def right_terms(b):
        for q in range(lanes // 512):
            part = dot(lbuf[...].reshape(seqs, wide), grs[b, :, q * 512 : q * 512 + 512])
            part = dot(part.astype(BF16), perm[...], 1, 1).astype(BF16)
            for o in range(per):
                for h in range(2):
                    gsend[b * per + o, h, :, q * 128 : q * 128 + 128] = part[
                        h * half_s : (h + 1) * half_s, o * 128 : o * 128 + 128]

        @pl.loop(0, 2 * per)
        def _(x):
            o, h = b * per + (x // 2 + r) % per, x % 2
            mine = (k * owners + o == r) & (h == k)

            @pl.when(mine)
            def _():
                pltpu.make_async_copy(gsend.at[o, h], gbuf.at[r], gsem.at[r]).start()

            @pl.when(jnp.logical_not(mine))
            def _():
                right_back(o, h).start()

    each_block(right_terms)

    if blocks > 1:
        gacc[...] = jnp.zeros(gacc.shape, F32)
        glacc[...] = jnp.zeros(glacc.shape, F32)

    half_w = gacc.shape[1]

    def weight_half(hh):
        at = pl.ds(pl.multiple_of(hh * half_w, half_w), half_w)
        val = dot(os[at, :], bd[...])
        if blocks == 1:
            gacc[hh] = val
        else:
            gacc[hh] += val

    weight_copy = remote(gacc.at[sib], wsib, wsem.at[0], wsem.at[1], r, sib)
    lane = lax.broadcasted_iota(jnp.int32, (128, 128), 1)

    def forward(b):
        if blocks > 1:
            fill_bd(b)
        for o in range(per):
            for h in range(2):
                landed(rbuf.at[b * per + o, h], rsem.at[b * per + o, h])
        for q in range(lanes // 512):
            cat = jnp.concatenate(
                [rbuf[b * per + o, :, :, q * 128 : q * 128 + 128].reshape(seqs, 128)
                 for o in range(per)], axis=1)
            rs[:, q * 512 : q * 512 + 512] = dot(cat, perm[...]).astype(BF16)

        @pl.loop(0, d2n // 2)
        def _(p):
            res = dot(lt[...], rs[:, pl.ds(pl.multiple_of(p * 256, 256), 256)]) * inv_seqs
            for u in range(2):
                for i in range(ires):
                    scr[i, pl.ds(2 * p + u, chan, stride=d2n), :] = res[
                        i * chan : (i + 1) * chan, u * 128 : u * 128 + 128]

        for i in range(ires):
            os[:, i * 128 : i * 128 + 128] = scr[i].astype(BF16)

        weight_half(sib)
        if blocks == 1:
            weight_copy.start()
        weight_half(k)

        @pl.loop(0, ires // 2)
        def _(p):
            res = dot(wt[...], os[:, pl.ds(pl.multiple_of(p * 256, 256), 256)])
            for u in range(2):
                both = jnp.where(
                    lane < 64, res[0:128, u * 128 : u * 128 + 128],
                    res[128:256, u * 128 : u * 128 + 128]).T
                pair_ref[2 * p + u, pl.ds(pl.multiple_of(b * 64, 64), 64), :] = (
                    both[0:64] + both[64:128] + bias_ref[...].astype(F32)).astype(BF16)

        val = dot(rs[...], grs[b], 1, 1)
        for h in range(2):
            if blocks == 1:
                glacc[h] = val[h * half_s : (h + 1) * half_s]
            else:
                glacc[h] += val[h * half_s : (h + 1) * half_s]

    each_block(forward)
    if blocks > 1:
        weight_copy.start()
    gl_copy = remote(glacc.at[sib], glsib, glsem.at[0], glsem.at[1], r, sib)
    gl_copy.start()

    weight_copy.wait_recv()
    slab = half_w // own
    wsend[...] = (gacc[k] + wsib[...]).astype(BF16).reshape(wsend.shape)

    def weight_send(p):
        return remote(wsend.at[p], wr.at[r], wssem.at[p], wrsem.at[r], p * stride, k)

    @pl.loop(0, own)
    def _(t):
        p = (r // stride + t) % own

        @pl.when(p * stride == r)
        def _():
            pltpu.make_async_copy(wsend.at[p], wr.at[r], wrsem.at[r]).start()

        @pl.when(p * stride != r)
        def _():
            weight_send(p).start()

    total = jnp.zeros((half_s, wide), F32)
    if rows <= 8:
        for q in range(rows):
            landed(gbuf.at[q], gsem.at[q])
            total = total + gbuf[q].astype(F32)
        gr_ref[...] = total * inv_seqs
    else:
        gr_ref[...] = total

        @pl.loop(0, rows)
        def _(q):
            landed(gbuf.at[q], gsem.at[q])
            gr_ref[...] += gbuf[q].astype(F32) * inv_seqs

    inv_rows = 1.0 / (ires * rows)
    me = r // stride

    def share(t):
        return remote(agbuf.at[k, me], agbuf.at[k, me], assem.at[t], asem.at[k, me], (r + t) % rows, k)

    def pass_on(p):
        return remote(agbuf.at[k, p], agbuf.at[k, p], fsem.at[p], asem.at[k, p], r, sib)

    def own_slice():
        def add(q, acc):
            landed(wr.at[q], wrsem.at[q])
            return acc + wr[q].astype(F32)

        agbuf[k, me] = lax.fori_loop(0, rows, add, jnp.zeros((slab, 256), F32)) * inv_rows
        pl.loop(1, rows)(lambda t: share(t).start())
        pass_on(me).start()

    if stride == 1:
        own_slice()
    else:
        pl.when(r % stride == 0)(own_slice)

    gl_copy.wait_recv()
    gl_ref[...] = (glacc[k] + glsib[...]) * inv_seqs

    def add_bias(q, acc):
        @pl.when(q != 2 * r + k)
        def _():
            landed(bbuf.at[q], bsem.at[q])

        return acc + bbuf[q]

    gb_ref[...] = lax.fori_loop(0, 2 * rows, add_bias, jnp.zeros(bsend.shape, F32)) * inv_rows

    @pl.loop(0, own)
    def _(t):
        p = (me + t) % own

        @pl.when(p * stride != r)
        def _():
            landed(agbuf.at[k, p], asem.at[k, p])
            pass_on(p).start()

    @pl.loop(0, own)
    def _(p):
        landed(agbuf.at[sib, p], asem.at[sib, p])

    whole = agbuf[...].reshape(2 * half_w, 256)
    gw_ref[pl.ds(0, 2 * half_w, stride=2), :] = whole[:, 0:128]
    gw_ref[pl.ds(1, 2 * half_w, stride=2), :] = whole[:, 128:256]

    left_copy.wait_send()

    @pl.when(kt != k)
    def _():
        remote(right_ref, rbuf.at[ol, k], rssem.at[0], rsem.at[ol, k], r, sib).wait_send()

    pl.loop(1, rows)(lambda t: right_copy(t).wait_send())
    pl.loop(1, 2 * rows)(lambda t: bias_copy(t).wait_send())

    @pl.loop(0, 2 * owners)
    def _(x):
        o, h = x // 2, x % 2

        @pl.when(jnp.logical_not((k * owners + o == r) & (h == k)))
        def _():
            right_back(o, h).wait_send()

    weight_copy.wait_send()
    gl_copy.wait_send()

    @pl.loop(0, own)
    def _(p):
        @pl.when(p * stride != r)
        def _():
            weight_send(p).wait_send()

    def shared():
        pl.loop(1, rows)(lambda t: share(t).wait_send())

    if stride == 1:
        shared()
    else:
        pl.when(r % stride == 0)(shared)
    pl.loop(0, own)(lambda p: pass_on(p).wait_send())


def local(rows, alignment_left, alignment_right, weight, pairwise_bias, cotangent):
    half_s, chan, ires = alignment_left.shape
    wide = chan * ires
    pair_dim = weight.shape[1]
    d2n = chan // 2
    own = min(rows, 8)
    owners = rows // 2
    blocks = owners * ires // 64
    half_w = chan * d2n // 2
    left = jnp.transpose(alignment_left, (0, 2, 1)).reshape(half_s, wide)
    right = alignment_right.reshape(half_s, wide)
    w = weight.reshape(chan * d2n, 2 * pair_dim)
    vmem, dma = pltpu.VMEM, pltpu.SemaphoreType.DMA
    lanes = d2n * 128
    pair, gl, gr, gw, gb = pl.pallas_call(
        functools.partial(kernel, rows, own),
        out_shape=(
            jax.ShapeDtypeStruct(cotangent.shape, BF16),
            jax.ShapeDtypeStruct((half_s, wide), F32),
            jax.ShapeDtypeStruct((half_s, wide), F32),
            jax.ShapeDtypeStruct((chan * chan, pair_dim), F32),
            jax.ShapeDtypeStruct((8, pair_dim), F32),
        ),
        in_specs=[pl.BlockSpec(memory_space=vmem)] * 5,
        out_specs=tuple([pl.BlockSpec(memory_space=vmem)] * 5),
        scratch_shapes=[
            vmem((2, half_s, wide), BF16),
            vmem((owners, 2, half_s, wide), BF16),
            vmem((512, 512), BF16),
            vmem((wide, 2 * half_s), BF16),
            vmem((2 * pair_dim, chan * d2n), BF16),
            vmem((ires * 128, 2 * pair_dim), BF16),
            vmem((ires, chan * d2n, 128), F32),
            vmem((blocks, wide, lanes), BF16),
            vmem((2 * half_s, lanes), BF16),
            vmem((chan * d2n, ires * 128), BF16),
            vmem((owners, 2, half_s, wide), BF16),
            vmem((rows, half_s, wide), BF16),
            vmem((2, half_w, 2 * pair_dim), F32),
            vmem((half_w, 2 * pair_dim), F32),
            vmem((own, half_w // own, 2 * pair_dim), BF16),
            vmem((rows, half_w // own, 2 * pair_dim), BF16),
            vmem((2, own, half_w // own, 2 * pair_dim), F32),
            vmem((2, half_s, wide), F32),
            vmem((half_s, wide), F32),
            vmem((8, pair_dim), F32),
            vmem((2 * rows, 8, pair_dim), F32),
            dma((2,)), dma((rows,)), dma((owners, 2)), dma((owners, 2)), dma((rows,)),
            dma((2,)), dma((own,)), dma((rows,)), dma((rows,)), dma((2, own)), dma((own,)),
            dma((2,)), dma((2 * rows,)), dma((2 * rows,)),
        ],
        compiler_params=pltpu.CompilerParams(
            collective_id=0, has_side_effects=True, vmem_limit_bytes=58 * 2**20),
    )(left, right, w, pairwise_bias.reshape(1, pair_dim), cotangent)
    gl = jnp.transpose(gl.reshape(half_s, ires, chan), (0, 2, 1))
    return pair, gl, gr.reshape(half_s, chan, ires), gw, gb[0]


def solution(mesh):
    in_specs = (
        P("col", None, ("grp", "row")),
        P("col", None, ("grp", "row")),
        P(),
        P(),
        P(("grp", "row"), "col", None),
    )
    out_specs = (
        P(("grp", "row"), "col", None),
        P("col", None, ("grp", "row")),
        P("col", None, ("grp", "row")),
        P("grp", None),
        P("grp"),
    )
    return jax.shard_map(
        functools.partial(local, mesh.shape["row"]), mesh=mesh,
        in_specs=in_specs, out_specs=out_specs, check_vma=False)
```

```python
import functools

import jax
import jax.numpy as jnp
from jax import lax
from jax.experimental import pallas as pl
from jax.experimental.pallas import tpu as pltpu
from jax.sharding import PartitionSpec as P

MESH = pl.DeviceIdType.MESH
F32, BF16 = jnp.float32, jnp.bfloat16


def dot(a, b, ca=1, cb=0):
    return lax.dot_general(a, b, (((ca,), (cb,)), ((), ())), preferred_element_type=F32)


def kernel(
    rows, own, left_ref, right_ref, w_ref, bias_ref, cot_ref,
    pair_ref, gl_ref, gr_ref, gw_ref, gb_ref,
    rsend, lsend, perm2, wf, w2, gls, lbuf, rbuf, perm, lt, wt, bd, scr, grs, rs, os, gsend, gbuf,
    gacc, wsib, wsend, wr, agbuf, glacc, glsib, bsend, bbuf,
    lsem, rssem, rsem, gssem, gsem, wsem, wssem, wrsem, assem, asem, fsem, glsem, bssem, bsem,
):
    g, r, k = lax.axis_index("grp"), lax.axis_index("row"), lax.axis_index("col")
    sib = 1 - k
    wide, half_s = left_ref.shape
    ires = cot_ref.shape[0]
    chan = wide // ires
    d2n = chan // 2
    seqs = 2 * half_s
    inv_seqs = 1.0 / seqs
    owners = rows // 2
    per = 64 // ires
    blocks = owners // per
    kt, ol = r // owners, r % owners
    stride = rows // own
    lanes = d2n * 128

    def remote(src, dst, ss, rs_, row, col):
        return pltpu.make_async_remote_copy(
            src_ref=src, dst_ref=dst, send_sem=ss, recv_sem=rs_,
            device_id=(g, row, col), device_id_type=MESH)

    def landed(ref, sem):
        pltpu.make_async_copy(ref, ref, sem).wait()

    barrier = pltpu.get_barrier_semaphore()

    @pl.loop(1, 2 * rows)
    def _(t):
        q = (2 * r + k + t) % (2 * rows)
        pl.semaphore_signal(barrier, inc=1, device_id=(g, q // 2, q % 2), device_id_type=MESH)

    rsend[...] = right_ref[...].astype(F32).T.astype(BF16)
    pl.semaphore_wait(barrier, 2 * rows - 1)

    def right_copy(t):
        return remote(rsend, rbuf.at[ol, k], rssem.at[t], rsem.at[ol, k], (r + t) % rows, kt)

    @pl.when(kt == k)
    def _():
        pltpu.make_async_copy(rsend, rbuf.at[ol, k], rsem.at[ol, k]).start()

    @pl.when(kt != k)
    def _():
        remote(rsend, rbuf.at[ol, k], rssem.at[0], rsem.at[ol, k], r, sib).start()

    @pl.loop(1, rows)
    def _(t):
        right_copy(t).start()

    pm = lax.broadcasted_iota(jnp.int32, (wide, wide), 0)
    pn = lax.broadcasted_iota(jnp.int32, (wide, wide), 1)
    perm2[...] = jnp.where((pm % ires) * chan + pm // ires == pn, 1.0, 0.0).astype(BF16)
    lsend[...] = dot(left_ref[...], perm2[...], 0, 0).astype(BF16)
    left_copy = remote(lsend, lbuf.at[k], lsem.at[0], lsem.at[1], r, sib)
    left_copy.start()

    bsend[...] = jnp.broadcast_to(
        jnp.sum(cot_ref[...].astype(F32), axis=(0, 1)).reshape(1, -1), bsend.shape)

    def bias_copy(t):
        q = (2 * r + k + t) % (2 * rows)
        return remote(bsend, bbuf.at[2 * r + k], bssem.at[t], bsem.at[2 * r + k], q // 2, q % 2)

    @pl.loop(1, 2 * rows)
    def _(t):
        bias_copy(t).start()

    bbuf[2 * r + k] = bsend[...]
    lbuf[k] = lsend[...]

    dd = 128 // ires
    pm = lax.broadcasted_iota(jnp.int32, perm.shape, 0)
    pn = lax.broadcasted_iota(jnp.int32, perm.shape, 1)
    goal = (pm % 128 // ires) * 64 + (pm // 128) * ires + pm % ires
    perm[...] = jnp.where(goal == pn, 1.0, 0.0).astype(BF16)
    wf[...] = w_ref[...].astype(F32)
    for u in range(2):
        part = wf[pl.ds(u, chan * d2n, stride=2), :]
        w2[:, u * 128 : u * 128 + 128] = part.astype(BF16)
        wt[u * 128 : u * 128 + 128, :] = part.T.astype(BF16)
    bd[...] = jnp.zeros(bd.shape, BF16)

    def fill_bd(b):
        for i in range(ires):
            piece = cot_ref[i, pl.ds(pl.multiple_of(b * 64, 64), 64), :]
            bd[i * 128 : i * 128 + 64, 0:128] = piece
            bd[i * 128 + 64 : i * 128 + 128, 128:256] = piece

    def each_block(fn):
        if blocks == 1:
            fn(0)
        else:
            pl.loop(0, blocks)(fn)

    def grads(b):
        fill_bd(b)

        @pl.loop(0, ires // 2)
        def _(p):
            res = dot(w2[...], bd[pl.ds(pl.multiple_of(p * 256, 256), 256), :], 1, 1)
            for u in range(2):
                scr[u] = res[:, u * 128 : u * 128 + 128]
            for u in range(2):
                at = pl.multiple_of((2 * p + u) * chan, chan)
                for q in range(d2n):
                    grs[b, pl.ds(at, chan), q * 128 : q * 128 + 128] = scr[
                        u, pl.ds(q, chan, stride=d2n), :].astype(BF16)

    each_block(grads)

    left_copy.wait_recv()
    lm = lbuf[...].reshape(seqs, wide)
    lt[...] = lm.astype(F32).T.astype(BF16)

    def right_back(o, h):
        return remote(gsend.at[o, h], gbuf.at[r], gssem.at[o, h], gsem.at[r], k * owners + o, h)

    def right_terms(b):
        for q in range(lanes // 512):
            part = dot(lbuf[...].reshape(seqs, wide), grs[b, :, q * 512 : q * 512 + 512])
            part = dot(part.astype(BF16), perm[...], 1, 1).astype(BF16)
            for o in range(per):
                for h in range(2):
                    gsend[b * per + o, h, :, q * 128 : q * 128 + 128] = part[
                        h * half_s : (h + 1) * half_s, o * 128 : o * 128 + 128]

        @pl.loop(0, 2 * per)
        def _(x):
            o, h = b * per + (x // 2 + r) % per, x % 2
            mine = (k * owners + o == r) & (h == k)

            @pl.when(mine)
            def _():
                pltpu.make_async_copy(gsend.at[o, h], gbuf.at[r], gsem.at[r]).start()

            @pl.when(jnp.logical_not(mine))
            def _():
                right_back(o, h).start()

    each_block(right_terms)

    if blocks > 1:
        gacc[...] = jnp.zeros(gacc.shape, F32)
        glacc[...] = jnp.zeros(glacc.shape, F32)

    half_w = gacc.shape[1]

    def weight_half(hh):
        at = pl.ds(pl.multiple_of(hh * half_w, half_w), half_w)
        val = dot(os[at, :], bd[...])
        if blocks == 1:
            gacc[hh] = val
        else:
            gacc[hh] += val

    weight_copy = remote(gacc.at[sib], wsib, wsem.at[0], wsem.at[1], r, sib)
    lane = lax.broadcasted_iota(jnp.int32, (128, 128), 1)

    def forward(b):
        if blocks > 1:
            fill_bd(b)
        for o in range(per):
            for h in range(2):
                landed(rbuf.at[b * per + o, h], rsem.at[b * per + o, h])
        for q in range(lanes // 512):
            cat = jnp.concatenate(
                [rbuf[b * per + o, :, :, q * 128 : q * 128 + 128].reshape(seqs, 128)
                 for o in range(per)], axis=1)
            rs[:, q * 512 : q * 512 + 512] = dot(cat, perm[...]).astype(BF16)

        @pl.loop(0, d2n // 2)
        def _(p):
            res = dot(lt[...], rs[:, pl.ds(pl.multiple_of(p * 256, 256), 256)]) * inv_seqs
            for u in range(2):
                for i in range(ires):
                    scr[i, pl.ds(2 * p + u, chan, stride=d2n), :] = res[
                        i * chan : (i + 1) * chan, u * 128 : u * 128 + 128]

        for i in range(ires):
            os[:, i * 128 : i * 128 + 128] = scr[i].astype(BF16)

        weight_half(sib)
        if blocks == 1:
            weight_copy.start()
        weight_half(k)

        @pl.loop(0, ires // 2)
        def _(p):
            res = dot(wt[...], os[:, pl.ds(pl.multiple_of(p * 256, 256), 256)])
            for u in range(2):
                both = jnp.where(
                    lane < 64, res[0:128, u * 128 : u * 128 + 128],
                    res[128:256, u * 128 : u * 128 + 128]).T
                pair_ref[2 * p + u, pl.ds(pl.multiple_of(b * 64, 64), 64), :] = (
                    both[0:64] + both[64:128] + bias_ref[...].astype(F32)).astype(BF16)

        val = dot(rs[...], grs[b], 1, 1)
        for h in range(2):
            if blocks == 1:
                glacc[h] = val[h * half_s : (h + 1) * half_s]
            else:
                glacc[h] += val[h * half_s : (h + 1) * half_s]

    each_block(forward)
    if blocks > 1:
        weight_copy.start()
    gl_copy = remote(glacc.at[sib], glsib, glsem.at[0], glsem.at[1], r, sib)
    gl_copy.start()

    weight_copy.wait_recv()
    slab = half_w // own
    wsend[...] = (gacc[k] + wsib[...]).astype(BF16).reshape(wsend.shape)

    def weight_send(p):
        return remote(wsend.at[p], wr.at[r], wssem.at[p], wrsem.at[r], p * stride, k)

    @pl.loop(0, own)
    def _(t):
        p = (r // stride + t) % own

        @pl.when(p * stride == r)
        def _():
            pltpu.make_async_copy(wsend.at[p], wr.at[r], wrsem.at[r]).start()

        @pl.when(p * stride != r)
        def _():
            weight_send(p).start()

    total = jnp.zeros((half_s, wide), F32)
    if rows <= 8:
        for q in range(rows):
            landed(gbuf.at[q], gsem.at[q])
            total = total + gbuf[q].astype(F32)
        gr_ref[...] = (total * inv_seqs).T
    else:
        gr_ref[...] = total.T

        @pl.loop(0, rows)
        def _(q):
            landed(gbuf.at[q], gsem.at[q])
            gr_ref[...] += (gbuf[q].astype(F32) * inv_seqs).T

    inv_rows = 1.0 / (ires * rows)
    me = r // stride

    def share(t):
        return remote(agbuf.at[k, me], agbuf.at[k, me], assem.at[t], asem.at[k, me], (r + t) % rows, k)

    def pass_on(p):
        return remote(agbuf.at[k, p], agbuf.at[k, p], fsem.at[p], asem.at[k, p], r, sib)

    def own_slice():
        def add(q, acc):
            landed(wr.at[q], wrsem.at[q])
            return acc + wr[q].astype(F32)

        agbuf[k, me] = lax.fori_loop(0, rows, add, jnp.zeros((slab, 256), F32)) * inv_rows
        pl.loop(1, rows)(lambda t: share(t).start())
        pass_on(me).start()

    if stride == 1:
        own_slice()
    else:
        pl.when(r % stride == 0)(own_slice)

    gl_copy.wait_recv()
    gls[...] = ((glacc[k] + glsib[...]) * inv_seqs).T
    for i in range(ires):
        gl_ref[pl.ds(i, chan, stride=ires), :] = gls[i * chan : (i + 1) * chan, :]

    def add_bias(q, acc):
        @pl.when(q != 2 * r + k)
        def _():
            landed(bbuf.at[q], bsem.at[q])

        return acc + bbuf[q]

    bias_sum = lax.fori_loop(0, 2 * rows, add_bias, jnp.zeros(bsend.shape, F32)) * inv_rows
    gb_ref[...] = bias_sum[0:1, :]

    @pl.loop(0, own)
    def _(t):
        p = (me + t) % own

        @pl.when(p * stride != r)
        def _():
            landed(agbuf.at[k, p], asem.at[k, p])
            pass_on(p).start()

    @pl.loop(0, own)
    def _(p):
        landed(agbuf.at[sib, p], asem.at[sib, p])

    whole = agbuf[...].reshape(2 * half_w, 256)
    gw_ref[pl.ds(0, 2 * half_w, stride=2), :] = whole[:, 0:128]
    gw_ref[pl.ds(1, 2 * half_w, stride=2), :] = whole[:, 128:256]

    left_copy.wait_send()

    @pl.when(kt != k)
    def _():
        remote(rsend, rbuf.at[ol, k], rssem.at[0], rsem.at[ol, k], r, sib).wait_send()

    pl.loop(1, rows)(lambda t: right_copy(t).wait_send())
    pl.loop(1, 2 * rows)(lambda t: bias_copy(t).wait_send())

    @pl.loop(0, 2 * owners)
    def _(x):
        o, h = x // 2, x % 2

        @pl.when(jnp.logical_not((k * owners + o == r) & (h == k)))
        def _():
            right_back(o, h).wait_send()

    weight_copy.wait_send()
    gl_copy.wait_send()

    @pl.loop(0, own)
    def _(p):
        @pl.when(p * stride != r)
        def _():
            weight_send(p).wait_send()

    def shared():
        pl.loop(1, rows)(lambda t: share(t).wait_send())

    if stride == 1:
        shared()
    else:
        pl.when(r % stride == 0)(shared)
    pl.loop(0, own)(lambda p: pass_on(p).wait_send())


def local(rows, alignment_left, alignment_right, weight, pairwise_bias, cotangent):
    half_s, chan, ires = alignment_left.shape
    wide = chan * ires
    pair_dim = weight.shape[1]
    d2n = chan // 2
    own = min(rows, 8)
    owners = rows // 2
    blocks = owners * ires // 64
    half_w = chan * d2n // 2
    left = jnp.transpose(alignment_left, (1, 2, 0)).reshape(wide, half_s)
    right = jnp.transpose(alignment_right, (1, 2, 0)).reshape(wide, half_s)
    vmem, dma = pltpu.VMEM, pltpu.SemaphoreType.DMA
    lanes = d2n * 128
    pair, gl, gr, gw, gb = pl.pallas_call(
        functools.partial(kernel, rows, own),
        out_shape=(
            jax.ShapeDtypeStruct(cotangent.shape, BF16),
            jax.ShapeDtypeStruct((wide, half_s), F32),
            jax.ShapeDtypeStruct((wide, half_s), F32),
            jax.ShapeDtypeStruct((chan * chan, pair_dim), F32),
            jax.ShapeDtypeStruct((1, pair_dim), F32),
        ),
        in_specs=[pl.BlockSpec(memory_space=vmem)] * 5,
        out_specs=tuple([pl.BlockSpec(memory_space=vmem)] * 5),
        scratch_shapes=[
            vmem((half_s, wide), BF16),
            vmem((half_s, wide), BF16),
            vmem((wide, wide), BF16),
            vmem((chan * chan, pair_dim), F32),
            vmem((chan * d2n, 2 * pair_dim), BF16),
            vmem((wide, half_s), F32),
            vmem((2, half_s, wide), BF16),
            vmem((owners, 2, half_s, wide), BF16),
            vmem((512, 512), BF16),
            vmem((wide, 2 * half_s), BF16),
            vmem((2 * pair_dim, chan * d2n), BF16),
            vmem((ires * 128, 2 * pair_dim), BF16),
            vmem((ires, chan * d2n, 128), F32),
            vmem((blocks, wide, lanes), BF16),
            vmem((2 * half_s, lanes), BF16),
            vmem((chan * d2n, ires * 128), BF16),
            vmem((owners, 2, half_s, wide), BF16),
            vmem((rows, half_s, wide), BF16),
            vmem((2, half_w, 2 * pair_dim), F32),
            vmem((half_w, 2 * pair_dim), F32),
            vmem((own, half_w // own, 2 * pair_dim), BF16),
            vmem((rows, half_w // own, 2 * pair_dim), BF16),
            vmem((2, own, half_w // own, 2 * pair_dim), F32),
            vmem((2, half_s, wide), F32),
            vmem((half_s, wide), F32),
            vmem((8, pair_dim), F32),
            vmem((2 * rows, 8, pair_dim), F32),
            dma((2,)), dma((rows,)), dma((owners, 2)), dma((owners, 2)), dma((rows,)),
            dma((2,)), dma((own,)), dma((rows,)), dma((rows,)), dma((2, own)), dma((own,)),
            dma((2,)), dma((2 * rows,)), dma((2 * rows,)),
        ],
        compiler_params=pltpu.CompilerParams(
            collective_id=0, has_side_effects=True, vmem_limit_bytes=58 * 2**20),
    )(left, right, weight, pairwise_bias.reshape(1, pair_dim), cotangent)
    gl, gr = (jnp.transpose(x.reshape(chan, ires, half_s), (2, 0, 1)) for x in (gl, gr))
    return pair, gl, gr, gw, gb.reshape(pair_dim)


def solution(mesh):
    in_specs = (
        P("col", None, ("grp", "row")),
        P("col", None, ("grp", "row")),
        P(),
        P(),
        P(("grp", "row"), "col", None),
    )
    out_specs = (
        P(("grp", "row"), "col", None),
        P("col", None, ("grp", "row")),
        P("col", None, ("grp", "row")),
        P("grp", None),
        P("grp"),
    )
    return jax.shard_map(
        functools.partial(local, mesh.shape["row"]), mesh=mesh,
        in_specs=in_specs, out_specs=out_specs, check_vma=False)
```

```python
import functools

import jax
import jax.numpy as jnp
from jax import lax
from jax.experimental import pallas as pl
from jax.experimental.pallas import tpu as pltpu
from jax.sharding import PartitionSpec as P

MESH = pl.DeviceIdType.MESH
F32, BF16 = jnp.float32, jnp.bfloat16


def dot(a, b, ca=1, cb=0):
    return lax.dot_general(a, b, (((ca,), (cb,)), ((), ())), preferred_element_type=F32)


def kernel(
    rows, own, left_ref, right_ref, w_ref, bias_ref, cot_ref,
    pair_ref, gl_ref, gr_ref, gw_ref, gb_ref,
    rsend, lsend, perm2, wf, w2, gls, lbuf, rbuf, perm, lt, wt, bd, scr, grs, rs, os, gsend, gbuf,
    gacc, wsib, wsend, wr, agbuf, glacc, glsib, bsend, bbuf,
    lsem, rssem, rsem, gssem, gsem, wsem, wssem, wrsem, assem, asem, fsem, glsem, bssem, bsem, hsem, gmid, gmsem, gm2sem,
):
    g, r, k = lax.axis_index("grp"), lax.axis_index("row"), lax.axis_index("col")
    sib = 1 - k
    wide, half_s = left_ref.shape
    ires = cot_ref.shape[0]
    chan = wide // ires
    d2n = chan // 2
    seqs = 2 * half_s
    inv_seqs = 1.0 / seqs
    owners = rows // 2
    per = 64 // ires
    blocks = owners // per
    kt, ol = r // owners, r % owners
    y = r % 2
    peer = r + 1 - 2 * y
    cols = rows // 2
    stride = rows // own
    lanes = d2n * 128

    def remote(src, dst, ss, rs_, row, col):
        return pltpu.make_async_remote_copy(
            src_ref=src, dst_ref=dst, send_sem=ss, recv_sem=rs_,
            device_id=(g, row, col), device_id_type=MESH)

    def landed(ref, sem):
        pltpu.make_async_copy(ref, ref, sem).wait()

    barrier = pltpu.get_barrier_semaphore()

    @pl.loop(1, 2 * rows)
    def _(t):
        q = (2 * r + k + t) % (2 * rows)
        pl.semaphore_signal(barrier, inc=1, device_id=(g, q // 2, q % 2), device_id_type=MESH)

    rsend[...] = right_ref[...].astype(F32).T.astype(BF16)
    pl.semaphore_wait(barrier, 2 * rows - 1)

    def right_copy(t):
        return remote(rsend, rbuf.at[ol, k], rssem.at[t], rsem.at[ol, k], (r + 2 * t) % rows, kt)

    @pl.when(kt == k)
    def _():
        pltpu.make_async_copy(rsend, rbuf.at[ol, k], rsem.at[ol, k]).start()

    @pl.when(kt != k)
    def _():
        remote(rsend, rbuf.at[ol, k], rssem.at[0], rsem.at[ol, k], r, sib).start()

    peer_copy = remote(rsend, rbuf.at[ol, k], rssem.at[cols], rsem.at[ol, k], peer, kt)
    peer_copy.start()

    @pl.loop(1, cols)
    def _(t):
        right_copy(t).start()

    def hand_on(x):
        o, h = 2 * (x // 2) + y, x % 2
        return remote(rbuf.at[o, h], rbuf.at[o, h], hsem.at[x], rsem.at[o, h], peer, k)

    def not_mine(x):
        return k * owners + 2 * (x // 2) + y != r

    def hand_all():
        @pl.loop(0, owners)
        def _(x):
            o, h = 2 * (x // 2) + y, x % 2
            landed(rbuf.at[o, h], rsem.at[o, h])

            @pl.when(not_mine(x))
            def _():
                hand_on(x).start()

    ibits, dbits = ires.bit_length() - 1, (128 // ires).bit_length() - 1
    pm = lax.broadcasted_iota(jnp.int32, (wide, wide), 0)
    pn = lax.broadcasted_iota(jnp.int32, (wide, wide), 1)
    goal = (pm & (ires - 1)) * chan + (pm >> ibits)
    perm2[...] = jnp.where(goal == pn, 1.0, 0.0).astype(BF16)
    lsend[...] = dot(left_ref[...], perm2[...], 0, 0).astype(BF16)
    left_copy = remote(lsend, lbuf.at[k], lsem.at[0], lsem.at[1], r, sib)
    left_copy.start()

    bsend[...] = jnp.broadcast_to(
        jnp.sum(cot_ref[...].astype(F32), axis=(0, 1)).reshape(1, -1), bsend.shape)

    def bias_copy(t):
        q = (2 * r + k + t) % (2 * rows)
        return remote(bsend, bbuf.at[2 * r + k], bssem.at[t], bsem.at[2 * r + k], q // 2, q % 2)

    @pl.loop(1, 2 * rows)
    def _(t):
        bias_copy(t).start()

    bbuf[2 * r + k] = bsend[...]
    lbuf[k] = lsend[...]

    pm = lax.broadcasted_iota(jnp.int32, perm.shape, 0)
    pn = lax.broadcasted_iota(jnp.int32, perm.shape, 1)
    goal = ((pm >> ibits) & (2**dbits - 1)) * 64 + (pm >> 7) * ires + (pm & (ires - 1))
    perm[...] = jnp.where(goal == pn, 1.0, 0.0).astype(BF16)
    wf[...] = w_ref[...].astype(F32)
    for u in range(2):
        part = wf[pl.ds(u, chan * d2n, stride=2), :]
        w2[:, u * 128 : u * 128 + 128] = part.astype(BF16)
        wt[u * 128 : u * 128 + 128, :] = part.T.astype(BF16)
    bd[...] = jnp.zeros(bd.shape, BF16)

    def fill_bd(b):
        for i in range(ires):
            piece = cot_ref[i, pl.ds(pl.multiple_of(b * 64, 64), 64), :]
            bd[i * 128 : i * 128 + 64, 0:128] = piece
            bd[i * 128 + 64 : i * 128 + 128, 128:256] = piece

    def each_block(fn):
        if blocks == 1:
            fn(0)
        else:
            pl.loop(0, blocks)(fn)

    def grads(b):
        fill_bd(b)

        @pl.loop(0, ires // 2)
        def _(p):
            res = dot(w2[...], bd[pl.ds(pl.multiple_of(p * 256, 256), 256), :], 1, 1)
            for u in range(2):
                scr[u] = res[:, u * 128 : u * 128 + 128]
            for u in range(2):
                at = pl.multiple_of((2 * p + u) * chan, chan)
                for q in range(d2n):
                    grs[b, pl.ds(at, chan), q * 128 : q * 128 + 128] = scr[
                        u, pl.ds(q, chan, stride=d2n), :].astype(BF16)

    each_block(grads)
    hand_all()

    left_copy.wait_recv()
    lm = lbuf[...].reshape(seqs, wide)
    lt[...] = lm.astype(F32).T.astype(BF16)

    def right_back(o, h):
        return remote(
            gsend.at[o, h], gbuf.at[r // 2], gssem.at[o, h], gsem.at[r // 2], k * owners + o, h)

    def pair_send(x):
        o, h = 2 * (x // 2) + 1 - y, x % 2
        return remote(gsend.at[o, h], gmid.at[x], gm2sem.at[x], gmsem.at[x], peer, k)

    def right_terms(b):
        for q in range(lanes // 512):
            part = dot(lbuf[...].reshape(seqs, wide), grs[b, :, q * 512 : q * 512 + 512])
            part = dot(part.astype(BF16), perm[...], 1, 1).astype(BF16)
            for o in range(per):
                for h in range(2):
                    gsend[b * per + o, h, :, q * 128 : q * 128 + 128] = part[
                        h * half_s : (h + 1) * half_s, o * 128 : o * 128 + 128]

        @pl.loop(0, per)
        def _(x):
            pair_send(b * per + x).start()

    each_block(right_terms)

    if blocks > 1:
        gacc[...] = jnp.zeros(gacc.shape, F32)
        glacc[...] = jnp.zeros(glacc.shape, F32)

    half_w = gacc.shape[1]

    def weight_half(hh):
        at = pl.ds(pl.multiple_of(hh * half_w, half_w), half_w)
        val = dot(os[at, :], bd[...])
        if blocks == 1:
            gacc[hh] = val
        else:
            gacc[hh] += val

    weight_copy = remote(gacc.at[sib], wsib, wsem.at[0], wsem.at[1], r, sib)
    lane = lax.broadcasted_iota(jnp.int32, (128, 128), 1)

    def forward(b):
        if blocks > 1:
            fill_bd(b)
        @pl.loop(0, per)
        def _(x):
            o, h = b * per + 2 * (x // 2) + 1 - y, x % 2
            landed(rbuf.at[o, h], rsem.at[o, h])

        for q in range(lanes // 512):
            cat = jnp.concatenate(
                [rbuf[b * per + o, :, :, q * 128 : q * 128 + 128].reshape(seqs, 128)
                 for o in range(per)], axis=1)
            rs[:, q * 512 : q * 512 + 512] = dot(cat, perm[...]).astype(BF16)

        if blocks == 1:
            pl.loop(0, owners)(right_sums)

        @pl.loop(0, d2n // 2)
        def _(p):
            res = dot(lt[...], rs[:, pl.ds(pl.multiple_of(p * 256, 256), 256)]) * inv_seqs
            for u in range(2):
                for i in range(ires):
                    scr[i, pl.ds(2 * p + u, chan, stride=d2n), :] = res[
                        i * chan : (i + 1) * chan, u * 128 : u * 128 + 128]

        for i in range(ires):
            os[:, i * 128 : i * 128 + 128] = scr[i].astype(BF16)

        weight_half(sib)
        if blocks == 1:
            weight_copy.start()
        weight_half(k)

        @pl.loop(0, ires // 2)
        def _(p):
            res = dot(wt[...], os[:, pl.ds(pl.multiple_of(p * 256, 256), 256)])
            for u in range(2):
                both = jnp.where(
                    lane < 64, res[0:128, u * 128 : u * 128 + 128],
                    res[128:256, u * 128 : u * 128 + 128]).T
                pair_ref[2 * p + u, pl.ds(pl.multiple_of(b * 64, 64), 64), :] = (
                    both[0:64] + both[64:128] + bias_ref[...].astype(F32)).astype(BF16)

        val = dot(rs[...], grs[b], 1, 1)
        for h in range(2):
            if blocks == 1:
                glacc[h] = val[h * half_s : (h + 1) * half_s]
            else:
                glacc[h] += val[h * half_s : (h + 1) * half_s]

    def right_sums(x):
        o, h = 2 * (x // 2) + y, x % 2
        landed(gmid.at[x], gmsem.at[x])
        gsend[o, h] = (gsend[o, h].astype(F32) + gmid[x].astype(F32)).astype(BF16)
        mine = (k * owners + o == r) & (h == k)

        @pl.when(mine)
        def _():
            pltpu.make_async_copy(gsend.at[o, h], gbuf.at[r // 2], gsem.at[r // 2]).start()

        @pl.when(jnp.logical_not(mine))
        def _():
            right_back(o, h).start()

    if blocks > 1:
        pl.loop(0, owners)(right_sums)
    each_block(forward)
    if blocks > 1:
        weight_copy.start()
    gl_copy = remote(glacc.at[sib], glsib, glsem.at[0], glsem.at[1], r, sib)
    gl_copy.start()

    weight_copy.wait_recv()
    slab = half_w // own
    wsend[...] = (gacc[k] + wsib[...]).astype(BF16).reshape(wsend.shape)

    def weight_send(p):
        return remote(wsend.at[p], wr.at[r], wssem.at[p], wrsem.at[r], p * stride, k)

    @pl.loop(0, own)
    def _(t):
        p = (r // stride + t) % own

        @pl.when(p * stride == r)
        def _():
            pltpu.make_async_copy(wsend.at[p], wr.at[r], wrsem.at[r]).start()

        @pl.when(p * stride != r)
        def _():
            weight_send(p).start()

    total = jnp.zeros((half_s, wide), F32)
    if rows <= 8:
        for q in range(cols):
            landed(gbuf.at[q], gsem.at[q])
            total = total + gbuf[q].astype(F32)
        gr_ref[...] = (total * inv_seqs).T
    else:
        gr_ref[...] = total.T

        @pl.loop(0, cols)
        def _(q):
            landed(gbuf.at[q], gsem.at[q])
            gr_ref[...] += (gbuf[q].astype(F32) * inv_seqs).T

    inv_rows = 1.0 / (ires * rows)
    me = r // stride

    def share(t):
        return remote(agbuf.at[k, me], agbuf.at[k, me], assem.at[t], asem.at[k, me], (r + t) % rows, k)

    def pass_on(p):
        return remote(agbuf.at[k, p], agbuf.at[k, p], fsem.at[p], asem.at[k, p], r, sib)

    def own_slice():
        def add(q, acc):
            landed(wr.at[q], wrsem.at[q])
            return acc + wr[q].astype(F32)

        mean = lax.fori_loop(0, rows, add, jnp.zeros((slab, 256), F32)) * inv_rows
        agbuf[k, me] = mean.astype(BF16)
        pl.loop(1, rows)(lambda t: share(t).start())
        pass_on(me).start()

    if stride == 1:
        own_slice()
    else:
        pl.when(r % stride == 0)(own_slice)

    gl_copy.wait_recv()
    gls[...] = ((glacc[k] + glsib[...]) * inv_seqs).T
    for i in range(ires):
        gl_ref[pl.ds(i, chan, stride=ires), :] = gls[i * chan : (i + 1) * chan, :]

    def add_bias(q, acc):
        @pl.when(q != 2 * r + k)
        def _():
            landed(bbuf.at[q], bsem.at[q])

        return acc + bbuf[q]

    bias_sum = lax.fori_loop(0, 2 * rows, add_bias, jnp.zeros(bsend.shape, F32)) * inv_rows
    gb_ref[...] = bias_sum[0:1, :]

    @pl.loop(0, own)
    def _(t):
        p = (me + t) % own

        @pl.when(p * stride != r)
        def _():
            landed(agbuf.at[k, p], asem.at[k, p])
            pass_on(p).start()

    @pl.loop(0, own)
    def _(p):
        landed(agbuf.at[sib, p], asem.at[sib, p])

    whole = agbuf[...].astype(F32).reshape(2 * half_w, 256)
    gw_ref[pl.ds(0, 2 * half_w, stride=2), :] = whole[:, 0:128]
    gw_ref[pl.ds(1, 2 * half_w, stride=2), :] = whole[:, 128:256]

    left_copy.wait_send()

    @pl.when(kt != k)
    def _():
        remote(rsend, rbuf.at[ol, k], rssem.at[0], rsem.at[ol, k], r, sib).wait_send()

    pl.loop(1, cols)(lambda t: right_copy(t).wait_send())
    peer_copy.wait_send()

    @pl.loop(0, owners)
    def _(x):
        @pl.when(not_mine(x))
        def _():
            hand_on(x).wait_send()

        pair_send(x).wait_send()

    pl.loop(1, 2 * rows)(lambda t: bias_copy(t).wait_send())

    @pl.loop(0, owners)
    def _(x):
        o, h = 2 * (x // 2) + y, x % 2

        @pl.when(jnp.logical_not((k * owners + o == r) & (h == k)))
        def _():
            right_back(o, h).wait_send()

    weight_copy.wait_send()
    gl_copy.wait_send()

    @pl.loop(0, own)
    def _(p):
        @pl.when(p * stride != r)
        def _():
            weight_send(p).wait_send()

    def shared():
        pl.loop(1, rows)(lambda t: share(t).wait_send())

    if stride == 1:
        shared()
    else:
        pl.when(r % stride == 0)(shared)
    pl.loop(0, own)(lambda p: pass_on(p).wait_send())


def copy_out(*refs):
    n = len(refs) // 2
    sems = refs[-1]
    copies = [pltpu.make_async_copy(refs[i], refs[n + i], sems.at[i]) for i in range(n)]
    for copy in copies:
        copy.start()
    for copy in copies:
        copy.wait()


def local(rows, alignment_left, alignment_right, weight, pairwise_bias, cotangent):
    half_s, chan, ires = alignment_left.shape
    wide = chan * ires
    pair_dim = weight.shape[1]
    d2n = chan // 2
    own = min(rows, 8)
    owners = rows // 2
    blocks = owners * ires // 64
    half_w = chan * d2n // 2
    left = jnp.transpose(alignment_left, (1, 2, 0)).reshape(wide, half_s)
    right = jnp.transpose(alignment_right, (1, 2, 0)).reshape(wide, half_s)
    vmem, dma = pltpu.VMEM, pltpu.SemaphoreType.DMA
    lanes = d2n * 128
    results = pl.pallas_call(
        functools.partial(kernel, rows, own),
        out_shape=(
            jax.ShapeDtypeStruct(cotangent.shape, BF16),
            jax.ShapeDtypeStruct((wide, half_s), F32),
            jax.ShapeDtypeStruct((wide, half_s), F32),
            jax.ShapeDtypeStruct((chan * chan, pair_dim), F32),
            jax.ShapeDtypeStruct((1, pair_dim), F32),
        ),
        in_specs=[pl.BlockSpec(memory_space=vmem)] * 5,
        out_specs=tuple([pl.BlockSpec(memory_space=vmem)] * 5),
        scratch_shapes=[
            vmem((half_s, wide), BF16),
            vmem((half_s, wide), BF16),
            vmem((wide, wide), BF16),
            vmem((chan * chan, pair_dim), F32),
            vmem((chan * d2n, 2 * pair_dim), BF16),
            vmem((wide, half_s), F32),
            vmem((2, half_s, wide), BF16),
            vmem((owners, 2, half_s, wide), BF16),
            vmem((512, 512), BF16),
            vmem((wide, 2 * half_s), BF16),
            vmem((2 * pair_dim, chan * d2n), BF16),
            vmem((ires * 128, 2 * pair_dim), BF16),
            vmem((ires, chan * d2n, 128), F32),
            vmem((blocks, wide, lanes), BF16),
            vmem((2 * half_s, lanes), BF16),
            vmem((chan * d2n, ires * 128), BF16),
            vmem((owners, 2, half_s, wide), BF16),
            vmem((owners, half_s, wide), BF16),
            vmem((2, half_w, 2 * pair_dim), F32),
            vmem((half_w, 2 * pair_dim), F32),
            vmem((own, half_w // own, 2 * pair_dim), BF16),
            vmem((rows, half_w // own, 2 * pair_dim), BF16),
            vmem((2, own, half_w // own, 2 * pair_dim), BF16),
            vmem((2, half_s, wide), F32),
            vmem((half_s, wide), F32),
            vmem((8, pair_dim), F32),
            vmem((2 * rows, 8, pair_dim), F32),
            dma((2,)), dma((rows,)), dma((owners, 2)), dma((owners, 2)), dma((rows,)),
            dma((2,)), dma((own,)), dma((rows,)), dma((rows,)), dma((2, own)), dma((own,)),
            dma((2,)), dma((2 * rows,)), dma((2 * rows,)), dma((owners,)),
            vmem((owners, half_s, wide), BF16),
            dma((owners,)), dma((owners,)),
        ],
        compiler_params=pltpu.CompilerParams(
            collective_id=0, has_side_effects=True, vmem_limit_bytes=58 * 2**20),
    )(left, right, weight, pairwise_bias.reshape(1, pair_dim), cotangent)
    pair, gl, gr, gw, gb = pl.pallas_call(
        copy_out,
        out_shape=tuple(jax.ShapeDtypeStruct(x.shape, x.dtype) for x in results),
        in_specs=[pl.BlockSpec(memory_space=pl.ANY)] * 5,
        out_specs=tuple([pl.BlockSpec(memory_space=pl.ANY)] * 5),
        scratch_shapes=[dma((5,))],
        compiler_params=pltpu.CompilerParams(vmem_limit_bytes=63 * 2**20),
    )(*results)
    gl, gr = (jnp.transpose(x.reshape(chan, ires, half_s), (2, 0, 1)) for x in (gl, gr))
    return pair, gl, gr, gw, gb.reshape(pair_dim)


def solution(mesh):
    in_specs = (
        P("col", None, ("grp", "row")),
        P("col", None, ("grp", "row")),
        P(),
        P(),
        P(("grp", "row"), "col", None),
    )
    out_specs = (
        P(("grp", "row"), "col", None),
        P("col", None, ("grp", "row")),
        P("col", None, ("grp", "row")),
        P("grp", None),
        P("grp"),
    )
    return jax.shard_map(
        functools.partial(local, mesh.shape["row"]), mesh=mesh,
        in_specs=in_specs, out_specs=out_specs, check_vma=False)
```

```python
import functools

import jax
import jax.numpy as jnp
from jax import lax
from jax.experimental import pallas as pl
from jax.experimental.pallas import tpu as pltpu
from jax.sharding import PartitionSpec as P

MESH = pl.DeviceIdType.MESH
F32, BF16 = jnp.float32, jnp.bfloat16


def dot(a, b, ca=1, cb=0):
    return lax.dot_general(a, b, (((ca,), (cb,)), ((), ())), preferred_element_type=F32)


def kernel(
    rows, own, left_ref, right_ref, w_ref, bias_ref, cot_ref,
    pair_ref, gl_ref, gr_ref, gw_ref, gb_ref,
    rsend, lsend, perm2, wf, w2, gls, lbuf, rbuf, perm, lt, wt, bd, scr, grs, rs, os, gsend, gbuf,
    gacc, wsib, wsend, wr, agbuf, glacc, glsib, bsend, bbuf,
    lsem, rssem, rsem, gssem, gsem, wsem, wssem, wrsem, assem, asem, fsem, glsem, bssem, bsem, hsem, gmid, gmsem, gm2sem,
):
    g, r, k = lax.axis_index("grp"), lax.axis_index("row"), lax.axis_index("col")
    sib = 1 - k
    wide, half_s = left_ref.shape
    ires = cot_ref.shape[0]
    chan = wide // ires
    d2n = chan // 2
    seqs = 2 * half_s
    inv_seqs = 1.0 / seqs
    owners = rows // 2
    per = 64 // ires
    blocks = owners // per
    kt, ol = r // owners, r % owners
    y = r % 2
    peer = r + 1 - 2 * y
    cols = rows // 2
    stride = rows // own
    lanes = d2n * 128

    def remote(src, dst, ss, rs_, row, col):
        return pltpu.make_async_remote_copy(
            src_ref=src, dst_ref=dst, send_sem=ss, recv_sem=rs_,
            device_id=(g, row, col), device_id_type=MESH)

    def landed(ref, sem):
        pltpu.make_async_copy(ref, ref, sem).wait()

    barrier = pltpu.get_barrier_semaphore()

    @pl.loop(1, 2 * rows)
    def _(t):
        q = (2 * r + k + t) % (2 * rows)
        pl.semaphore_signal(barrier, inc=1, device_id=(g, q // 2, q % 2), device_id_type=MESH)

    rsend[...] = right_ref[...].astype(F32).T.astype(BF16)
    ibits, dbits = ires.bit_length() - 1, (128 // ires).bit_length() - 1
    pm = lax.broadcasted_iota(jnp.int32, (wide, wide), 0)
    pn = lax.broadcasted_iota(jnp.int32, (wide, wide), 1)
    goal = (pm & (ires - 1)) * chan + (pm >> ibits)
    perm2[...] = jnp.where(goal == pn, 1.0, 0.0).astype(BF16)
    lsend[...] = dot(left_ref[...], perm2[...], 0, 0).astype(BF16)
    pl.semaphore_wait(barrier, 2 * rows - 1)

    def right_copy(t):
        return remote(rsend, rbuf.at[ol, k], rssem.at[t], rsem.at[ol, k], (r + 2 * t) % rows, kt)

    @pl.when(kt == k)
    def _():
        pltpu.make_async_copy(rsend, rbuf.at[ol, k], rsem.at[ol, k]).start()

    @pl.when(kt != k)
    def _():
        remote(rsend, rbuf.at[ol, k], rssem.at[0], rsem.at[ol, k], r, sib).start()

    peer_copy = remote(rsend, rbuf.at[ol, k], rssem.at[cols], rsem.at[ol, k], peer, kt)

    @pl.loop(1, cols)
    def _(t):
        right_copy(t).start()

    peer_copy.start()

    def hand_on(x):
        o, h = 2 * (x // 2) + y, x % 2
        return remote(rbuf.at[o, h], rbuf.at[o, h], hsem.at[x], rsem.at[o, h], peer, k)

    def not_mine(x):
        return k * owners + 2 * (x // 2) + y != r

    def hand_all():
        @pl.loop(0, owners)
        def _(x):
            o, h = 2 * (x // 2) + y, x % 2
            landed(rbuf.at[o, h], rsem.at[o, h])

            @pl.when(not_mine(x))
            def _():
                hand_on(x).start()

    left_copy = remote(lsend, lbuf.at[k], lsem.at[0], lsem.at[1], r, sib)
    left_copy.start()

    bsend[...] = jnp.broadcast_to(
        jnp.sum(cot_ref[...].astype(F32), axis=(0, 1)).reshape(1, -1), bsend.shape)

    def bias_copy(t):
        q = (2 * r + k + t) % (2 * rows)
        return remote(bsend, bbuf.at[2 * r + k], bssem.at[t], bsem.at[2 * r + k], q // 2, q % 2)

    @pl.loop(1, 2 * rows)
    def _(t):
        bias_copy(t).start()

    bbuf[2 * r + k] = bsend[...]
    lbuf[k] = lsend[...]

    pm = lax.broadcasted_iota(jnp.int32, perm.shape, 0)
    pn = lax.broadcasted_iota(jnp.int32, perm.shape, 1)
    goal = ((pm >> ibits) & (2**dbits - 1)) * 64 + (pm >> 7) * ires + (pm & (ires - 1))
    perm[...] = jnp.where(goal == pn, 1.0, 0.0).astype(BF16)
    wf[...] = w_ref[...].astype(F32)
    for u in range(2):
        part = wf[pl.ds(u, chan * d2n, stride=2), :]
        w2[:, u * 128 : u * 128 + 128] = part.astype(BF16)
        wt[u * 128 : u * 128 + 128, :] = part.T.astype(BF16)
    bd[...] = jnp.zeros(bd.shape, BF16)

    def fill_bd(b):
        for i in range(ires):
            piece = cot_ref[i, pl.ds(pl.multiple_of(b * 64, 64), 64), :]
            bd[i * 128 : i * 128 + 64, 0:128] = piece
            bd[i * 128 + 64 : i * 128 + 128, 128:256] = piece

    def each_block(fn):
        if blocks == 1:
            fn(0)
        else:
            pl.loop(0, blocks)(fn)

    def grads(b):
        fill_bd(b)

        def step(p):
            res = dot(w2[...], bd[pl.ds(pl.multiple_of(p * 256, 256), 256), :], 1, 1)
            for u in range(2):
                scr[u] = res[:, u * 128 : u * 128 + 128]
            for u in range(2):
                at = pl.multiple_of((2 * p + u) * chan, chan)
                for q in range(d2n):
                    grs[b, pl.ds(at, chan), q * 128 : q * 128 + 128] = scr[
                        u, pl.ds(q, chan, stride=d2n), :].astype(BF16)

        pl.loop(0, ires // 4)(step)
        if blocks == 1:
            hand_all()
        pl.loop(ires // 4, ires // 2)(step)

    each_block(grads)
    if blocks > 1:
        hand_all()

    left_copy.wait_recv()
    lm = lbuf[...].reshape(seqs, wide)
    lt[...] = lm.astype(F32).T.astype(BF16)

    def right_back(o, h):
        return remote(
            gsend.at[o, h], gbuf.at[r // 2], gssem.at[o, h], gsem.at[r // 2], k * owners + o, h)

    def pair_send(x):
        o, h = 2 * (x // 2) + 1 - y, x % 2
        return remote(gsend.at[o, h], gmid.at[x], gm2sem.at[x], gmsem.at[x], peer, k)

    def right_terms(b):
        for q in range(lanes // 512):
            part = dot(lbuf[...].reshape(seqs, wide), grs[b, :, q * 512 : q * 512 + 512])
            part = dot(part.astype(BF16), perm[...], 1, 1).astype(BF16)
            for o in range(per):
                for h in range(2):
                    gsend[b * per + o, h, :, q * 128 : q * 128 + 128] = part[
                        h * half_s : (h + 1) * half_s, o * 128 : o * 128 + 128]

        @pl.loop(0, per)
        def _(x):
            pair_send(b * per + x).start()

    each_block(right_terms)

    if blocks > 1:
        gacc[...] = jnp.zeros(gacc.shape, F32)
        glacc[...] = jnp.zeros(glacc.shape, F32)

    half_w = gacc.shape[1]

    def weight_half(hh):
        at = pl.ds(pl.multiple_of(hh * half_w, half_w), half_w)
        val = dot(os[at, :], bd[...])
        if blocks == 1:
            gacc[hh] = val
        else:
            gacc[hh] += val

    weight_copy = remote(gacc.at[sib], wsib, wsem.at[0], wsem.at[1], r, sib)
    lane = lax.broadcasted_iota(jnp.int32, (128, 128), 1)

    def forward(b):
        if blocks > 1:
            fill_bd(b)
        @pl.loop(0, per)
        def _(x):
            o, h = b * per + 2 * (x // 2) + 1 - y, x % 2
            landed(rbuf.at[o, h], rsem.at[o, h])

        for q in range(lanes // 512):
            cat = jnp.concatenate(
                [rbuf[b * per + o, :, :, q * 128 : q * 128 + 128].reshape(seqs, 128)
                 for o in range(per)], axis=1)
            rs[:, q * 512 : q * 512 + 512] = dot(cat, perm[...]).astype(BF16)

        @pl.loop(0, d2n // 2)
        def _(p):
            res = dot(lt[...], rs[:, pl.ds(pl.multiple_of(p * 256, 256), 256)]) * inv_seqs
            for u in range(2):
                for i in range(ires):
                    scr[i, pl.ds(2 * p + u, chan, stride=d2n), :] = res[
                        i * chan : (i + 1) * chan, u * 128 : u * 128 + 128]

        for i in range(ires):
            os[:, i * 128 : i * 128 + 128] = scr[i].astype(BF16)

        weight_half(sib)
        if blocks == 1:
            weight_copy.start()
        weight_half(k)
        if blocks == 1:
            pl.loop(0, owners)(right_sums)

        @pl.loop(0, ires // 2)
        def _(p):
            res = dot(wt[...], os[:, pl.ds(pl.multiple_of(p * 256, 256), 256)])
            for u in range(2):
                both = jnp.where(
                    lane < 64, res[0:128, u * 128 : u * 128 + 128],
                    res[128:256, u * 128 : u * 128 + 128]).T
                pair_ref[2 * p + u, pl.ds(pl.multiple_of(b * 64, 64), 64), :] = (
                    both[0:64] + both[64:128] + bias_ref[...].astype(F32)).astype(BF16)

        val = dot(rs[...], grs[b], 1, 1)
        for h in range(2):
            if blocks == 1:
                glacc[h] = val[h * half_s : (h + 1) * half_s]
            else:
                glacc[h] += val[h * half_s : (h + 1) * half_s]

    def right_sums(x):
        o, h = 2 * (x // 2) + y, x % 2
        landed(gmid.at[x], gmsem.at[x])
        gsend[o, h] = (gsend[o, h].astype(F32) + gmid[x].astype(F32)).astype(BF16)
        mine = (k * owners + o == r) & (h == k)

        @pl.when(mine)
        def _():
            pltpu.make_async_copy(gsend.at[o, h], gbuf.at[r // 2], gsem.at[r // 2]).start()

        @pl.when(jnp.logical_not(mine))
        def _():
            right_back(o, h).start()

    if blocks > 1:
        pl.loop(0, owners)(right_sums)
    each_block(forward)
    if blocks > 1:
        weight_copy.start()
    gl_copy = remote(glacc.at[sib], glsib, glsem.at[0], glsem.at[1], r, sib)
    gl_copy.start()

    weight_copy.wait_recv()
    slab = half_w // own
    wsend[...] = (gacc[k] + wsib[...]).astype(BF16).reshape(wsend.shape)

    def weight_send(p):
        return remote(wsend.at[p], wr.at[r], wssem.at[p], wrsem.at[r], p * stride, k)

    @pl.loop(0, own)
    def _(t):
        p = (r // stride + t) % own

        @pl.when(p * stride == r)
        def _():
            pltpu.make_async_copy(wsend.at[p], wr.at[r], wrsem.at[r]).start()

        @pl.when(p * stride != r)
        def _():
            weight_send(p).start()

    total = jnp.zeros((half_s, wide), F32)
    if rows <= 8:
        for q in range(cols):
            landed(gbuf.at[q], gsem.at[q])
            total = total + gbuf[q].astype(F32)
        gr_ref[...] = (total * inv_seqs).T
    else:
        gr_ref[...] = total.T

        @pl.loop(0, cols)
        def _(q):
            landed(gbuf.at[q], gsem.at[q])
            gr_ref[...] += (gbuf[q].astype(F32) * inv_seqs).T

    inv_rows = 1.0 / (ires * rows)
    me = r // stride

    def share(t):
        return remote(agbuf.at[k, me], agbuf.at[k, me], assem.at[t], asem.at[k, me], (r + t) % rows, k)

    def pass_on(p):
        return remote(agbuf.at[k, p], agbuf.at[k, p], fsem.at[p], asem.at[k, p], r, sib)

    def own_slice():
        def add(q, acc):
            landed(wr.at[q], wrsem.at[q])
            return acc + wr[q].astype(F32)

        mean = lax.fori_loop(0, rows, add, jnp.zeros((slab, 256), F32)) * inv_rows
        agbuf[k, me] = mean.astype(BF16)
        pl.loop(1, rows)(lambda t: share(t).start())
        pass_on(me).start()

    if stride == 1:
        own_slice()
    else:
        pl.when(r % stride == 0)(own_slice)

    gl_copy.wait_recv()
    gls[...] = ((glacc[k] + glsib[...]) * inv_seqs).T
    for i in range(ires):
        gl_ref[pl.ds(i, chan, stride=ires), :] = gls[i * chan : (i + 1) * chan, :]

    def add_bias(q, acc):
        @pl.when(q != 2 * r + k)
        def _():
            landed(bbuf.at[q], bsem.at[q])

        return acc + bbuf[q]

    bias_sum = lax.fori_loop(0, 2 * rows, add_bias, jnp.zeros(bsend.shape, F32)) * inv_rows
    gb_ref[...] = bias_sum[0:1, :]

    @pl.loop(0, own)
    def _(t):
        p = (me + t) % own

        @pl.when(p * stride != r)
        def _():
            landed(agbuf.at[k, p], asem.at[k, p])
            pass_on(p).start()

    @pl.loop(0, own)
    def _(p):
        landed(agbuf.at[sib, p], asem.at[sib, p])

    whole = agbuf[...].astype(F32).reshape(2 * half_w, 256)
    gw_ref[pl.ds(0, 2 * half_w, stride=2), :] = whole[:, 0:128]
    gw_ref[pl.ds(1, 2 * half_w, stride=2), :] = whole[:, 128:256]

    left_copy.wait_send()

    @pl.when(kt != k)
    def _():
        remote(rsend, rbuf.at[ol, k], rssem.at[0], rsem.at[ol, k], r, sib).wait_send()

    pl.loop(1, cols)(lambda t: right_copy(t).wait_send())
    peer_copy.wait_send()

    @pl.loop(0, owners)
    def _(x):
        @pl.when(not_mine(x))
        def _():
            hand_on(x).wait_send()

        pair_send(x).wait_send()

    pl.loop(1, 2 * rows)(lambda t: bias_copy(t).wait_send())

    @pl.loop(0, owners)
    def _(x):
        o, h = 2 * (x // 2) + y, x % 2

        @pl.when(jnp.logical_not((k * owners + o == r) & (h == k)))
        def _():
            right_back(o, h).wait_send()

    weight_copy.wait_send()
    gl_copy.wait_send()

    @pl.loop(0, own)
    def _(p):
        @pl.when(p * stride != r)
        def _():
            weight_send(p).wait_send()

    def shared():
        pl.loop(1, rows)(lambda t: share(t).wait_send())

    if stride == 1:
        shared()
    else:
        pl.when(r % stride == 0)(shared)
    pl.loop(0, own)(lambda p: pass_on(p).wait_send())


def copy_out(*refs):
    n = len(refs) // 2
    for i in range(n):
        refs[n + i][...] = refs[i][...]


def local(rows, alignment_left, alignment_right, weight, pairwise_bias, cotangent):
    half_s, chan, ires = alignment_left.shape
    wide = chan * ires
    pair_dim = weight.shape[1]
    d2n = chan // 2
    own = min(rows, 8)
    owners = rows // 2
    blocks = owners * ires // 64
    half_w = chan * d2n // 2
    left = jnp.transpose(alignment_left, (1, 2, 0)).reshape(wide, half_s)
    right = jnp.transpose(alignment_right, (1, 2, 0)).reshape(wide, half_s)
    vmem, dma = pltpu.VMEM, pltpu.SemaphoreType.DMA
    lanes = d2n * 128
    results = pl.pallas_call(
        functools.partial(kernel, rows, own),
        out_shape=(
            jax.ShapeDtypeStruct(cotangent.shape, BF16),
            jax.ShapeDtypeStruct((wide, half_s), F32),
            jax.ShapeDtypeStruct((wide, half_s), F32),
            jax.ShapeDtypeStruct((chan * chan, pair_dim), F32),
            jax.ShapeDtypeStruct((1, pair_dim), F32),
        ),
        in_specs=[pl.BlockSpec(memory_space=vmem)] * 5,
        out_specs=tuple([pl.BlockSpec(memory_space=vmem)] * 5),
        scratch_shapes=[
            vmem((half_s, wide), BF16),
            vmem((half_s, wide), BF16),
            vmem((wide, wide), BF16),
            vmem((chan * chan, pair_dim), F32),
            vmem((chan * d2n, 2 * pair_dim), BF16),
            vmem((wide, half_s), F32),
            vmem((2, half_s, wide), BF16),
            vmem((owners, 2, half_s, wide), BF16),
            vmem((512, 512), BF16),
            vmem((wide, 2 * half_s), BF16),
            vmem((2 * pair_dim, chan * d2n), BF16),
            vmem((ires * 128, 2 * pair_dim), BF16),
            vmem((ires, chan * d2n, 128), F32),
            vmem((blocks, wide, lanes), BF16),
            vmem((2 * half_s, lanes), BF16),
            vmem((chan * d2n, ires * 128), BF16),
            vmem((owners, 2, half_s, wide), BF16),
            vmem((owners, half_s, wide), BF16),
            vmem((2, half_w, 2 * pair_dim), F32),
            vmem((half_w, 2 * pair_dim), F32),
            vmem((own, half_w // own, 2 * pair_dim), BF16),
            vmem((rows, half_w // own, 2 * pair_dim), BF16),
            vmem((2, own, half_w // own, 2 * pair_dim), BF16),
            vmem((2, half_s, wide), F32),
            vmem((half_s, wide), F32),
            vmem((8, pair_dim), F32),
            vmem((2 * rows, 8, pair_dim), F32),
            dma((2,)), dma((rows,)), dma((owners, 2)), dma((owners, 2)), dma((rows,)),
            dma((2,)), dma((own,)), dma((rows,)), dma((rows,)), dma((2, own)), dma((own,)),
            dma((2,)), dma((2 * rows,)), dma((2 * rows,)), dma((owners,)),
            vmem((owners, half_s, wide), BF16),
            dma((owners,)), dma((owners,)),
        ],
        compiler_params=pltpu.CompilerParams(
            collective_id=0, has_side_effects=True, vmem_limit_bytes=58 * 2**20),
    )(left, right, weight, pairwise_bias.reshape(1, pair_dim), cotangent)
    pair, gl, gr, gw, gb = pl.pallas_call(
        copy_out,
        out_shape=tuple(jax.ShapeDtypeStruct(x.shape, x.dtype) for x in results),
        in_specs=[pl.BlockSpec(memory_space=vmem)] * 5,
        out_specs=tuple([pl.BlockSpec(memory_space=vmem)] * 5),
        compiler_params=pltpu.CompilerParams(vmem_limit_bytes=58 * 2**20),
    )(*results)
    gl, gr = (jnp.transpose(x.reshape(chan, ires, half_s), (2, 0, 1)) for x in (gl, gr))
    return pair, gl, gr, gw, gb.reshape(pair_dim)


def solution(mesh):
    in_specs = (
        P("col", None, ("grp", "row")),
        P("col", None, ("grp", "row")),
        P(),
        P(),
        P(("grp", "row"), "col", None),
    )
    out_specs = (
        P(("grp", "row"), "col", None),
        P("col", None, ("grp", "row")),
        P("col", None, ("grp", "row")),
        P("grp", None),
        P("grp"),
    )
    return jax.shard_map(
        functools.partial(local, mesh.shape["row"]), mesh=mesh,
        in_specs=in_specs, out_specs=out_specs, check_vma=False)
```

```python
import functools

import jax
import jax.numpy as jnp
from jax import lax
from jax.experimental import pallas as pl
from jax.experimental.pallas import tpu as pltpu
from jax.sharding import PartitionSpec as P

MESH = pl.DeviceIdType.MESH
F32, BF16 = jnp.float32, jnp.bfloat16


def dot(a, b, ca=1, cb=0):
    return lax.dot_general(a, b, (((ca,), (cb,)), ((), ())), preferred_element_type=F32)


def kernel(
    rows, own, left_ref, right_ref, w_ref, bias_ref, cot_ref,
    pair_ref, gl_ref, gr_ref, gw_ref, gb_ref,
    rsend, lsend, perm2, wf, w2, gls, lbuf, rbuf, perm, lt, wt, bd, scr, grs, rs, os, gsend, gbuf,
    gacc, wsib, wsend, wr, agbuf, glacc, glsib, bsend, bbuf,
    lsem, rssem, rsem, gssem, gsem, wsem, wssem, wrsem, assem, asem, fsem, glsem, bssem, bsem, hsem, gmid, gmsem, gm2sem,
):
    g, r, k = lax.axis_index("grp"), lax.axis_index("row"), lax.axis_index("col")
    sib = 1 - k
    wide, half_s = left_ref.shape
    ires = cot_ref.shape[0]
    chan = wide // ires
    d2n = chan // 2
    seqs = 2 * half_s
    inv_seqs = 1.0 / seqs
    owners = rows // 2
    per = 64 // ires
    blocks = owners // per
    kt, ol = r // owners, r % owners
    y = r % 2
    peer = r + 1 - 2 * y
    cols = rows // 2
    stride = rows // own
    lanes = d2n * 128

    def remote(src, dst, ss, rs_, row, col):
        return pltpu.make_async_remote_copy(
            src_ref=src, dst_ref=dst, send_sem=ss, recv_sem=rs_,
            device_id=(g, row, col), device_id_type=MESH)

    def landed(ref, sem):
        pltpu.make_async_copy(ref, ref, sem).wait()

    barrier = pltpu.get_barrier_semaphore()

    @pl.loop(1, 2 * rows)
    def _(t):
        q = (2 * r + k + t) % (2 * rows)
        pl.semaphore_signal(barrier, inc=1, device_id=(g, q // 2, q % 2), device_id_type=MESH)

    rsend[...] = right_ref[...].astype(F32).T.astype(BF16)
    ibits, dbits = ires.bit_length() - 1, (128 // ires).bit_length() - 1
    pm = lax.broadcasted_iota(jnp.int32, (wide, wide), 0)
    pn = lax.broadcasted_iota(jnp.int32, (wide, wide), 1)
    goal = (pm & (ires - 1)) * chan + (pm >> ibits)
    perm2[...] = jnp.where(goal == pn, 1.0, 0.0).astype(BF16)
    lsend[...] = dot(left_ref[...], perm2[...], 0, 0).astype(BF16)
    pl.semaphore_wait(barrier, 2 * rows - 1)

    def right_copy(t):
        return remote(rsend, rbuf.at[ol, k], rssem.at[t], rsem.at[ol, k], (r + 2 * t) % rows, kt)

    @pl.when(kt == k)
    def _():
        pltpu.make_async_copy(rsend, rbuf.at[ol, k], rsem.at[ol, k]).start()

    @pl.when(kt != k)
    def _():
        remote(rsend, rbuf.at[ol, k], rssem.at[0], rsem.at[ol, k], r, sib).start()

    peer_copy = remote(rsend, rbuf.at[ol, k], rssem.at[cols], rsem.at[ol, k], peer, kt)

    @pl.loop(1, cols)
    def _(t):
        right_copy(t).start()

    peer_copy.start()

    def hand_on(x):
        o, h = 2 * (x // 2) + y, x % 2
        return remote(rbuf.at[o, h], rbuf.at[o, h], hsem.at[x], rsem.at[o, h], peer, k)

    def not_mine(x):
        return k * owners + 2 * (x // 2) + y != r

    def hand_all():
        @pl.loop(0, owners)
        def _(x):
            o, h = 2 * (x // 2) + y, x % 2
            landed(rbuf.at[o, h], rsem.at[o, h])

            @pl.when(not_mine(x))
            def _():
                hand_on(x).start()

    left_copy = remote(lsend, lbuf.at[k], lsem.at[0], lsem.at[1], r, sib)
    left_copy.start()

    bsend[...] = jnp.broadcast_to(
        jnp.sum(cot_ref[...].astype(F32), axis=(0, 1)).reshape(1, -1), bsend.shape)

    def bias_copy(t):
        q = (2 * r + k + t) % (2 * rows)
        return remote(bsend, bbuf.at[2 * r + k], bssem.at[t], bsem.at[2 * r + k], q // 2, q % 2)

    @pl.loop(1, 2 * rows)
    def _(t):
        bias_copy(t).start()

    bbuf[2 * r + k] = bsend[...]
    lbuf[k] = lsend[...]

    pm = lax.broadcasted_iota(jnp.int32, perm.shape, 0)
    pn = lax.broadcasted_iota(jnp.int32, perm.shape, 1)
    goal = ((pm >> ibits) & (2**dbits - 1)) * 64 + (pm >> 7) * ires + (pm & (ires - 1))
    perm[...] = jnp.where(goal == pn, 1.0, 0.0).astype(BF16)
    wf[...] = w_ref[...].astype(F32)
    for u in range(2):
        part = wf[pl.ds(u, chan * d2n, stride=2), :]
        w2[:, u * 128 : u * 128 + 128] = part.astype(BF16)
        wt[u * 128 : u * 128 + 128, :] = part.T.astype(BF16)
    bd[...] = jnp.zeros(bd.shape, BF16)

    def fill_bd(b):
        for i in range(ires):
            piece = cot_ref[i, pl.ds(pl.multiple_of(b * 64, 64), 64), :]
            bd[i * 128 : i * 128 + 64, 0:128] = piece
            bd[i * 128 + 64 : i * 128 + 128, 128:256] = piece

    def each_block(fn):
        if blocks == 1:
            fn(0)
        else:
            pl.loop(0, blocks)(fn)

    def grads(b):
        fill_bd(b)

        def step(p):
            res = dot(w2[...], bd[pl.ds(pl.multiple_of(p * 256, 256), 256), :], 1, 1)
            for u in range(2):
                scr[u] = res[:, u * 128 : u * 128 + 128]
            for u in range(2):
                at = pl.multiple_of((2 * p + u) * chan, chan)
                for q in range(d2n):
                    grs[b, pl.ds(at, chan), q * 128 : q * 128 + 128] = scr[
                        u, pl.ds(q, chan, stride=d2n), :].astype(BF16)

        pl.loop(0, ires // 4)(step)
        if blocks == 1:
            hand_all()
        pl.loop(ires // 4, ires // 2)(step)

    each_block(grads)
    if blocks > 1:
        hand_all()

    left_copy.wait_recv()
    lm = lbuf[...].reshape(seqs, wide)
    lt[...] = lm.astype(F32).T.astype(BF16)

    def right_back(o, h):
        return remote(
            gsend.at[o, h], gbuf.at[r // 2], gssem.at[o, h], gsem.at[r // 2], k * owners + o, h)

    def pair_send(x):
        o, h = 2 * (x // 2) + 1 - y, x % 2
        return remote(gsend.at[o, h], gmid.at[x], gm2sem.at[x], gmsem.at[x], peer, k)

    def right_terms(b):
        for q in range(lanes // 512):
            part = dot(lbuf[...].reshape(seqs, wide), grs[b, :, q * 512 : q * 512 + 512])
            part = dot(part.astype(BF16), perm[...], 1, 1).astype(BF16)
            for o in range(per):
                for h in range(2):
                    gsend[b * per + o, h, :, q * 128 : q * 128 + 128] = part[
                        h * half_s : (h + 1) * half_s, o * 128 : o * 128 + 128]

        @pl.loop(0, per)
        def _(x):
            pair_send(b * per + x).start()

    each_block(right_terms)

    if blocks > 1:
        gacc[...] = jnp.zeros(gacc.shape, F32)
        glacc[...] = jnp.zeros(glacc.shape, F32)

    half_w = gacc.shape[1]

    def weight_half(hh):
        at = pl.ds(pl.multiple_of(hh * half_w, half_w), half_w)
        val = dot(os[at, :], bd[...])
        if blocks == 1:
            gacc[hh] = val
        else:
            gacc[hh] += val

    weight_copy = remote(gacc.at[sib], wsib, wsem.at[0], wsem.at[1], r, sib)
    lane = lax.broadcasted_iota(jnp.int32, (128, 128), 1)

    def forward(b):
        if blocks > 1:
            fill_bd(b)
        @pl.loop(0, per)
        def _(x):
            o, h = b * per + 2 * (x // 2) + 1 - y, x % 2
            landed(rbuf.at[o, h], rsem.at[o, h])

        for q in range(lanes // 512):
            cat = jnp.concatenate(
                [rbuf[b * per + o, :, :, q * 128 : q * 128 + 128].reshape(seqs, 128)
                 for o in range(per)], axis=1)
            rs[:, q * 512 : q * 512 + 512] = dot(cat, perm[...]).astype(BF16)

        @pl.loop(0, d2n // 2)
        def _(p):
            res = dot(lt[...], rs[:, pl.ds(pl.multiple_of(p * 256, 256), 256)]) * inv_seqs
            for u in range(2):
                for i in range(ires):
                    scr[i, pl.ds(2 * p + u, chan, stride=d2n), :] = res[
                        i * chan : (i + 1) * chan, u * 128 : u * 128 + 128]

        for i in range(ires):
            os[:, i * 128 : i * 128 + 128] = scr[i].astype(BF16)

        weight_half(sib)
        if blocks == 1:
            weight_copy.start()
        weight_half(k)
        if blocks == 1:
            pl.loop(0, owners)(right_sums)

        @pl.loop(0, ires // 2)
        def _(p):
            res = dot(wt[...], os[:, pl.ds(pl.multiple_of(p * 256, 256), 256)])
            for u in range(2):
                both = jnp.where(
                    lane < 64, res[0:128, u * 128 : u * 128 + 128],
                    res[128:256, u * 128 : u * 128 + 128]).T
                pair_ref[2 * p + u, pl.ds(pl.multiple_of(b * 64, 64), 64), :] = (
                    both[0:64] + both[64:128] + bias_ref[...].astype(F32)).astype(BF16)

        val = dot(rs[...], grs[b], 1, 1)
        for h in range(2):
            if blocks == 1:
                glacc[h] = val[h * half_s : (h + 1) * half_s]
            else:
                glacc[h] += val[h * half_s : (h + 1) * half_s]

    def right_sums(x):
        o, h = 2 * (x // 2) + y, x % 2
        landed(gmid.at[x], gmsem.at[x])
        gsend[o, h] = (gsend[o, h].astype(F32) + gmid[x].astype(F32)).astype(BF16)
        mine = (k * owners + o == r) & (h == k)

        @pl.when(mine)
        def _():
            pltpu.make_async_copy(gsend.at[o, h], gbuf.at[r // 2], gsem.at[r // 2]).start()

        @pl.when(jnp.logical_not(mine))
        def _():
            right_back(o, h).start()

    if blocks > 1:
        pl.loop(0, owners)(right_sums)
    each_block(forward)
    if blocks > 1:
        weight_copy.start()
    gl_copy = remote(glacc.at[sib], glsib, glsem.at[0], glsem.at[1], r, sib)
    gl_copy.start()

    weight_copy.wait_recv()
    slab = half_w // own
    wsend[...] = (gacc[k] + wsib[...]).astype(BF16).reshape(wsend.shape)

    def weight_send(p):
        return remote(wsend.at[p], wr.at[r], wssem.at[p], wrsem.at[r], p * stride, k)

    @pl.loop(0, own)
    def _(t):
        p = (r // stride + t) % own

        @pl.when(p * stride == r)
        def _():
            pltpu.make_async_copy(wsend.at[p], wr.at[r], wrsem.at[r]).start()

        @pl.when(p * stride != r)
        def _():
            weight_send(p).start()

    inv_rows = 1.0 / (ires * rows)
    me = r // stride

    def share(t):
        return remote(agbuf.at[k, me], agbuf.at[k, me], assem.at[t], asem.at[k, me], (r + t) % rows, k)

    def pass_on(p):
        return remote(agbuf.at[k, p], agbuf.at[k, p], fsem.at[p], asem.at[k, p], r, sib)

    def own_slice():
        def add(q, acc):
            landed(wr.at[q], wrsem.at[q])
            return acc + wr[q].astype(F32)

        mean = lax.fori_loop(0, rows, add, jnp.zeros((slab, 256), F32)) * inv_rows
        agbuf[k, me] = mean.astype(BF16)
        pl.loop(1, rows)(lambda t: share(t).start())
        pass_on(me).start()

    if stride == 1:
        own_slice()
    else:
        pl.when(r % stride == 0)(own_slice)

    gl_copy.wait_recv()
    gls[...] = ((glacc[k] + glsib[...]) * inv_seqs).T
    for i in range(ires):
        gl_ref[pl.ds(i, chan, stride=ires), :] = gls[i * chan : (i + 1) * chan, :]

    def add_bias(q, acc):
        @pl.when(q != 2 * r + k)
        def _():
            landed(bbuf.at[q], bsem.at[q])

        return acc + bbuf[q]

    bias_sum = lax.fori_loop(0, 2 * rows, add_bias, jnp.zeros(bsend.shape, F32)) * inv_rows
    gb_ref[...] = bias_sum[0:1, :]

    @pl.loop(0, own)
    def _(t):
        p = (me + t) % own

        @pl.when(p * stride != r)
        def _():
            landed(agbuf.at[k, p], asem.at[k, p])
            pass_on(p).start()

    total = jnp.zeros((half_s, wide), F32)
    if rows <= 8:
        for q in range(cols):
            landed(gbuf.at[q], gsem.at[q])
            total = total + gbuf[q].astype(F32)
        gr_ref[...] = (total * inv_seqs).T
    else:
        gr_ref[...] = total.T

        @pl.loop(0, cols)
        def _(q):
            landed(gbuf.at[q], gsem.at[q])
            gr_ref[...] += (gbuf[q].astype(F32) * inv_seqs).T

    @pl.loop(0, own)
    def _(p):
        landed(agbuf.at[sib, p], asem.at[sib, p])

    whole = agbuf[...].astype(F32).reshape(2 * half_w, 256)
    gw_ref[pl.ds(0, 2 * half_w, stride=2), :] = whole[:, 0:128]
    gw_ref[pl.ds(1, 2 * half_w, stride=2), :] = whole[:, 128:256]

    left_copy.wait_send()

    @pl.when(kt != k)
    def _():
        remote(rsend, rbuf.at[ol, k], rssem.at[0], rsem.at[ol, k], r, sib).wait_send()

    pl.loop(1, cols)(lambda t: right_copy(t).wait_send())
    peer_copy.wait_send()

    @pl.loop(0, owners)
    def _(x):
        @pl.when(not_mine(x))
        def _():
            hand_on(x).wait_send()

        pair_send(x).wait_send()

    pl.loop(1, 2 * rows)(lambda t: bias_copy(t).wait_send())

    @pl.loop(0, owners)
    def _(x):
        o, h = 2 * (x // 2) + y, x % 2

        @pl.when(jnp.logical_not((k * owners + o == r) & (h == k)))
        def _():
            right_back(o, h).wait_send()

    weight_copy.wait_send()
    gl_copy.wait_send()

    @pl.loop(0, own)
    def _(p):
        @pl.when(p * stride != r)
        def _():
            weight_send(p).wait_send()

    def shared():
        pl.loop(1, rows)(lambda t: share(t).wait_send())

    if stride == 1:
        shared()
    else:
        pl.when(r % stride == 0)(shared)
    pl.loop(0, own)(lambda p: pass_on(p).wait_send())


def copy_out(*refs):
    n = len(refs) // 2
    for i in range(n):
        refs[n + i][...] = refs[i][...]


def local(rows, alignment_left, alignment_right, weight, pairwise_bias, cotangent):
    half_s, chan, ires = alignment_left.shape
    wide = chan * ires
    pair_dim = weight.shape[1]
    d2n = chan // 2
    own = min(rows, 8)
    owners = rows // 2
    blocks = owners * ires // 64
    half_w = chan * d2n // 2
    left = jnp.transpose(alignment_left, (1, 2, 0)).reshape(wide, half_s)
    right = jnp.transpose(alignment_right, (1, 2, 0)).reshape(wide, half_s)
    vmem, dma = pltpu.VMEM, pltpu.SemaphoreType.DMA
    lanes = d2n * 128
    results = pl.pallas_call(
        functools.partial(kernel, rows, own),
        out_shape=(
            jax.ShapeDtypeStruct(cotangent.shape, BF16),
            jax.ShapeDtypeStruct((wide, half_s), F32),
            jax.ShapeDtypeStruct((wide, half_s), F32),
            jax.ShapeDtypeStruct((chan * chan, pair_dim), F32),
            jax.ShapeDtypeStruct((1, pair_dim), F32),
        ),
        in_specs=[pl.BlockSpec(memory_space=vmem)] * 5,
        out_specs=tuple([pl.BlockSpec(memory_space=vmem)] * 5),
        scratch_shapes=[
            vmem((half_s, wide), BF16),
            vmem((half_s, wide), BF16),
            vmem((wide, wide), BF16),
            vmem((chan * chan, pair_dim), F32),
            vmem((chan * d2n, 2 * pair_dim), BF16),
            vmem((wide, half_s), F32),
            vmem((2, half_s, wide), BF16),
            vmem((owners, 2, half_s, wide), BF16),
            vmem((512, 512), BF16),
            vmem((wide, 2 * half_s), BF16),
            vmem((2 * pair_dim, chan * d2n), BF16),
            vmem((ires * 128, 2 * pair_dim), BF16),
            vmem((ires, chan * d2n, 128), F32),
            vmem((blocks, wide, lanes), BF16),
            vmem((2 * half_s, lanes), BF16),
            vmem((chan * d2n, ires * 128), BF16),
            vmem((owners, 2, half_s, wide), BF16),
            vmem((owners, half_s, wide), BF16),
            vmem((2, half_w, 2 * pair_dim), F32),
            vmem((half_w, 2 * pair_dim), F32),
            vmem((own, half_w // own, 2 * pair_dim), BF16),
            vmem((rows, half_w // own, 2 * pair_dim), BF16),
            vmem((2, own, half_w // own, 2 * pair_dim), BF16),
            vmem((2, half_s, wide), F32),
            vmem((half_s, wide), F32),
            vmem((8, pair_dim), F32),
            vmem((2 * rows, 8, pair_dim), F32),
            dma((2,)), dma((rows,)), dma((owners, 2)), dma((owners, 2)), dma((rows,)),
            dma((2,)), dma((own,)), dma((rows,)), dma((rows,)), dma((2, own)), dma((own,)),
            dma((2,)), dma((2 * rows,)), dma((2 * rows,)), dma((owners,)),
            vmem((owners, half_s, wide), BF16),
            dma((owners,)), dma((owners,)),
        ],
        compiler_params=pltpu.CompilerParams(
            collective_id=0, has_side_effects=True, vmem_limit_bytes=58 * 2**20),
    )(left, right, weight, pairwise_bias.reshape(1, pair_dim), cotangent)
    pair, gl, gr, gw, gb = pl.pallas_call(
        copy_out,
        out_shape=tuple(jax.ShapeDtypeStruct(x.shape, x.dtype) for x in results),
        in_specs=[pl.BlockSpec(memory_space=vmem)] * 5,
        out_specs=tuple([pl.BlockSpec(memory_space=vmem)] * 5),
        compiler_params=pltpu.CompilerParams(vmem_limit_bytes=58 * 2**20),
    )(*results)
    gl, gr = (jnp.transpose(x.reshape(chan, ires, half_s), (2, 0, 1)) for x in (gl, gr))
    return pair, gl, gr, gw, gb.reshape(pair_dim)


def solution(mesh):
    in_specs = (
        P("col", None, ("grp", "row")),
        P("col", None, ("grp", "row")),
        P(),
        P(),
        P(("grp", "row"), "col", None),
    )
    out_specs = (
        P(("grp", "row"), "col", None),
        P("col", None, ("grp", "row")),
        P("col", None, ("grp", "row")),
        P("grp", None),
        P("grp"),
    )
    return jax.shard_map(
        functools.partial(local, mesh.shape["row"]), mesh=mesh,
        in_specs=in_specs, out_specs=out_specs, check_vma=False)
```
